32 devices in a mesh: gr: 8 (over z, core), gc: 4 (over y, x).
Axes of the slice: x: 2, y: 2, z: 4, core: 2. Of those that a mesh axis runs over, the one named last changes fastest.
Arguments:
- out_grad: bfloat16 [16384, 512], P(('gr', 'gc')), may hold values from -6 to 6
- preactivation_state: bfloat16 [16384, 512], P(('gr', 'gc')), may hold values from -6 to 6
- features: bfloat16 [16384, 512], P(('gc', 'gr')), may hold values from -6 to 6
- weight: bfloat16 [512, 512], replicated, may hold values from -0.25 to 0.25
- block_values: bfloat16 [8, 4, 152, 128, 128], P('gr', 'gc'), may hold values from -0.1875 to 0.1875
- block_rows: int32 [8, 4, 152], P('gr', 'gc'), may hold values from 0 to 15, as said below
- block_cols: int32 [8, 4, 152], P('gr', 'gc'), may hold values from 0 to 31, as said below
- block_counts: int32 [8, 4], P('gr', 'gc'), may hold values from 1 to 152, as said below
Outputs:
- input_grad: bfloat16 [16384, 512], P(('gc', 'gr'))
- weight_grad: float32 [512, 512], replicated
The draws below stay inside these ranges and needn't reach their ends.
Inputs may be any that keep to these rules, and one draw needn't show every extreme that they name: `block_rows`: block row within a tile; some entry equals 15. `block_cols`: block column within a tile; some entry equals 31. `block_counts`: slots from this count on are unused; some tile uses all 152 slots.
All inputs are finite; a program needn't handle non-finite values.
Results may differ from the reference program's by a relative error of at most 0.014.
Values may be sent and summed in bfloat16 or wider, within the bound.
No kernel may reach another device: no remote copies, remote signals or barrier semaphores. Data moves between devices by JAX's collectives and lax.ppermute only.
A program may use at most 128 MiB of HBM per device.

```python
import jax
import jax.numpy as jnp
from jax import lax

D = 512
BLOCK = 128
ROWS_DEV = 512
BMAX = 152
NODES = 16384
ROW_BLOCKS = 16
COL_BLOCKS = 32
N_GR = 8
N_GC = 4


def draw_block_counts(key, part):
    first, second, third = jax.random.split(jax.random.fold_in(key, 11), 3)
    left = jax.random.randint(first, (N_GR, N_GC), 1, BMAX + 1)
    right = jax.random.randint(second, (N_GR, N_GC), 1, BMAX + 1)
    counts = (left * right + BMAX - 1) // BMAX
    peak = jax.random.randint(third, (), 0, N_GR * N_GC)
    places = jnp.arange(N_GR * N_GC).reshape(N_GR, N_GC)
    return jnp.where(places == peak, BMAX, counts).astype(jnp.int32)


def draw_block_rows(key, part):
    picks = jax.random.randint(jax.random.fold_in(key, 12), (N_GR, N_GC, BMAX), 0, ROW_BLOCKS)
    return picks.at[0, 0, 0].set(ROW_BLOCKS - 1).astype(jnp.int32)


def draw_block_cols(key, part):
    picks = jax.random.randint(jax.random.fold_in(key, 13), (N_GR, N_GC, BMAX), 0, COL_BLOCKS)
    return picks.at[0, 0, 0].set(COL_BLOCKS - 1).astype(jnp.int32)


def strengthened(array, own_key, source, target, parts, factor):
    def block_of(axis_at):
        return (jnp.arange(array.shape[axis_at]) // (array.shape[axis_at] // parts)).reshape((-1,) + (1,) * (array.ndim - 1 - axis_at))

    near = jax.random.permutation(own_key, parts)[block_of(target)]
    far = (block_of(target) + parts // 2) % parts
    return jnp.where((block_of(source) == near) | (block_of(source) == far), factor * array, array)


def block_scale(key, extent, cuts, smallest, largest):
    level, own = 1.0, jax.random.fold_in(key, 6)
    for position, shards_of in cuts:
        steps = jnp.exp(jax.random.uniform(jax.random.fold_in(own, position), (shards_of,), jnp.float32, smallest / len(cuts), largest / len(cuts)))
        level = level * jnp.repeat(steps, extent[position] // shards_of).reshape([-1 if axis == position else 1 for axis in range(len(extent))])
    return level


def scatter_about(key, shape, deviation, reach, pieces=(), held_as=jnp.bfloat16):
    result = deviation * jax.random.normal(key, shape, jnp.float32)
    if pieces:
        result = result * block_scale(key, shape, pieces, -0.22, 0.18)
    return jnp.clip(result, -reach, reach).astype(held_as)


def gaussian_with(key, dims, scale, bound, cuts, heavy, kind=jnp.bfloat16):
    drawn = scale * jax.random.normal(key, dims, jnp.float32)
    if cuts:
        drawn = drawn * block_scale(key, dims, cuts, -0.22, 0.18)
    return jnp.clip(strengthened(drawn, jax.random.fold_in(key, 3), *heavy), -bound, bound).astype(kind)


def setup_inputs(seed: int = 0) -> dict:
    arg_keys = jax.random.split(jax.random.key(seed), 9)
    out_grad = scatter_about(arg_keys[0], (NODES, D), 1.0, 6.0, ((0, 32),))
    preactivation_state = scatter_about(arg_keys[1], (NODES, D), 1.0, 6.0, ((0, 32),))
    features = gaussian_with(arg_keys[2], (NODES, D), 1.0, 6.0, ((0, 32),), (0, 1, 32, 2.75))
    weight = scatter_about(arg_keys[3], (D, D), D ** -0.5, 0.25)
    block_values = scatter_about(arg_keys[4], (N_GR, N_GC, BMAX, BLOCK, BLOCK), (BLOCK * 8) ** -0.5, 0.1875, ((0, 8), (1, 4)))
    block_rows = draw_block_rows(jax.random.fold_in(arg_keys[8], 71), 0)
    block_cols = draw_block_cols(jax.random.fold_in(arg_keys[8], 71), 0)
    block_counts = draw_block_counts(jax.random.fold_in(arg_keys[8], 71), 0)
    return {"out_grad": out_grad, "preactivation_state": preactivation_state, "features": features, "weight": weight, "block_values": block_values, "block_rows": block_rows, "block_cols": block_cols, "block_counts": block_counts}


def tile_partial(masked, block_values, block_rows, block_cols, block_counts, tile_row, tile_col):
    tile_height = ROWS_DEV * N_GC
    offset = (tile_row * tile_height).astype(jnp.int32)
    rows_now = lax.dynamic_slice_in_dim(masked, offset, tile_height, 0).reshape(ROW_BLOCKS, BLOCK, D)
    current_values = block_values[tile_row, tile_col]
    selected_entries = rows_now[block_rows[tile_row, tile_col]]
    contribution = jnp.einsum('yql,yqa->yla', current_values.astype(jnp.float32), selected_entries.astype(jnp.float32))
    active = jnp.arange(BMAX) < block_counts[tile_row, tile_col]
    contribution = jnp.where(active[:, None, None], contribution, jnp.zeros_like(contribution))
    value_partial_sum = jnp.zeros((COL_BLOCKS, BLOCK, D), jnp.float32).at[block_cols[tile_row, tile_col]].add(contribution)
    return value_partial_sum.reshape(COL_BLOCKS * BLOCK, D).astype(jnp.bfloat16)


def reference(out_grad, preactivation_state, features, weight, block_values, block_rows, block_cols, block_counts):
    masked = jnp.where(preactivation_state > 0, out_grad, jnp.zeros_like(out_grad)).astype(jnp.bfloat16)

    def column_sum(tile_col):
        def add_tile(tile_row, total):
            return total + tile_partial(masked, block_values, block_rows, block_cols, block_counts, tile_row, tile_col).astype(jnp.float32)
        return lax.fori_loop(0, N_GR, add_tile, jnp.zeros((ROWS_DEV * N_GR, D), jnp.float32))

    totals = lax.map(column_sum, jnp.arange(N_GC, dtype=jnp.int32))
    spread = totals.reshape(NODES, D).astype(jnp.bfloat16)
    input_grad = jnp.dot(spread, weight.T, preferred_element_type=jnp.float32).astype(jnp.bfloat16)
    weight_grad = jnp.dot(features.T, spread, preferred_element_type=jnp.float32) * (NODES ** -0.5)
    return input_grad, weight_grad
```

```python
import functools

import jax
import jax.numpy as jnp
from jax import lax
from jax.experimental import pallas as pl
from jax.experimental.pallas import tpu as pltpu
from jax.sharding import PartitionSpec as P

QUAD = 4
UNROLL = 2
VMEM = pl.BlockSpec(memory_space=pltpu.VMEM)
SMEM = pl.BlockSpec(memory_space=pltpu.SMEM)
F32 = jnp.float32
BF16 = jnp.bfloat16


def params(mib=48):
    return pltpu.CompilerParams(vmem_limit_bytes=mib * 2**20)


def xor_permute(array, axis, mask):
    size = lax.axis_size(axis)
    return lax.ppermute(array, axis, [(i, i ^ mask) for i in range(size)])


def bit_reversed(index, bits):
    result = 0
    for bit in range(bits):
        result = result + ((index >> bit) & 1) * (1 << (bits - 1 - bit))
    return result


def pack_kernel(
    sizes, rows_ref, cols_ref, count_ref, values_ref, packed_ref, row_at_ref, col_at_ref, groups_ref, place
):
    n_gr, capacity, columns, limit, block, per_part, bits = sizes
    me_gr, me_gc = lax.axis_index("gr"), lax.axis_index("gc")
    count = count_ref[0]

    def row_offset(row):
        return (((row // per_part) ^ me_gc) * per_part + row % per_part) * block

    def col_offset(col):
        part = bit_reversed((col // per_part) ^ me_gr, bits)
        return (part * per_part + col % per_part) * block

    def store(slot, tile):
        lane = pl.multiple_of((slot % QUAD) * block, block)
        packed_ref[slot // QUAD, :, pl.ds(lane, block)] = tile

    def clear(c, carry):
        place[c] = 0
        return carry

    lax.fori_loop(0, columns + 1, clear, 0)

    def tally(s, carry):
        c = cols_ref[s]
        place[c] = place[c] + 1
        return carry

    lax.fori_loop(0, count, tally, 0)

    def open_column(c, group):
        held = place[c]
        taken = (held + QUAD - 1) // QUAD
        place[c] = group * QUAD

        def label(g, carry):
            col_at_ref[g] = col_offset(c)
            return carry

        lax.fori_loop(group, group + taken, label, 0)

        def pad(slot, carry):
            row_at_ref[slot] = 0
            store(slot, jnp.zeros((block, block), BF16))
            return carry

        lax.fori_loop(group * QUAD + held, (group + taken) * QUAD, pad, 0)
        return group + taken

    total = lax.fori_loop(0, columns, open_column, 0)
    groups_ref[0] = total
    for extra in range(UNROLL):
        col_at_ref[total + extra] = columns * block
        for j in range(QUAD):
            row_at_ref[(total + extra) * QUAD + j] = 0
    place[columns] = (limit + UNROLL - 1) * QUAD

    def insert(step, carry):
        for u in range(4):
            s = jnp.minimum(step * 4 + u, capacity - 1)
            active = step * 4 + u < count
            c = jnp.where(active, cols_ref[s], columns)
            slot = place[c]
            place[c] = slot + active.astype(jnp.int32)
            row_at_ref[slot] = row_offset(rows_ref[s])
            store(slot, values_ref[s].T)
        return carry

    lax.fori_loop(0, (count + 3) // 4, insert, 0)


def pack(values, rows, cols, count, n_gr, columns, per_part):
    capacity, block, _ = values.shape
    limit = (capacity + columns * (QUAD - 1)) // QUAD
    bits = n_gr.bit_length() - 1
    room = limit + UNROLL
    sizes = (n_gr, capacity, columns, limit, block, per_part, bits)
    return pl.pallas_call(
        functools.partial(pack_kernel, sizes),
        out_shape=(
            jax.ShapeDtypeStruct((room, block, QUAD * block), BF16),
            jax.ShapeDtypeStruct((room * QUAD,), jnp.int32),
            jax.ShapeDtypeStruct((room,), jnp.int32),
            jax.ShapeDtypeStruct((1,), jnp.int32),
        ),
        in_specs=[SMEM, SMEM, SMEM, VMEM],
        out_specs=(VMEM, SMEM, SMEM, SMEM),
        scratch_shapes=[pltpu.SMEM((columns + 1,), jnp.int32)],
        compiler_params=params(),
        cost_estimate=pl.CostEstimate(flops=0, bytes_accessed=18_000_000, transcendentals=0),
        name="pack_blocks",
    )(rows, cols, count, values)


def spmm_kernel(n_gc, packed_ref, row_at_ref, col_at_ref, groups_ref, *refs):
    parts, (keep_ref, send_ref, stacked, total) = refs[:n_gc], refs[n_gc:]
    part_rows = parts[0].shape[0]
    block = packed_ref.shape[1]
    half = keep_ref.shape[0]
    for k in range(n_gc):
        stacked[k * part_rows : (k + 1) * part_rows] = parts[k][...]
    total[...] = jnp.zeros_like(total)

    def step(i, carry):
        products = []
        for u in range(UNROLL):
            g = i * UNROLL + u
            chosen = [
                stacked[pl.ds(pl.multiple_of(row_at_ref[g * QUAD + j], block), block)] for j in range(QUAD)
            ]
            products.append(
                jnp.dot(packed_ref[g], jnp.concatenate(chosen, axis=0), preferred_element_type=F32)
            )
        for u in range(UNROLL):
            place = pl.ds(pl.multiple_of(col_at_ref[i * UNROLL + u], block), block)
            total[place] = total[place] + products[u]
        return carry

    lax.fori_loop(0, (groups_ref[0] + UNROLL - 1) // UNROLL, step, 0)
    keep_ref[...] = total[:half].astype(BF16)
    send_ref[...] = total[half : 2 * half].astype(BF16)


def spmm(packed, parts, out_rows):
    n_gc = len(parts)
    part_rows, width = parts[0].shape
    block = packed[0].shape[1]
    half = jax.ShapeDtypeStruct((out_rows // 2, width), BF16)
    return pl.pallas_call(
        functools.partial(spmm_kernel, n_gc),
        out_shape=(half, half),
        in_specs=[VMEM, SMEM, SMEM, SMEM] + [VMEM] * n_gc,
        out_specs=(VMEM, VMEM),
        scratch_shapes=[
            pltpu.VMEM((n_gc * part_rows, width), BF16),
            pltpu.VMEM((out_rows + block, width), F32),
        ],
        compiler_params=params(),
        cost_estimate=pl.CostEstimate(
            flops=2 * 64 * 4 * block * block * width, bytes_accessed=10_000_000, transcendentals=0
        ),
        name="tile_partial",
    )(*packed, *parts)


def finish_kernel(n_gc, n_chunks, *refs):
    keeps, recvs = refs[:n_chunks], refs[n_chunks : 2 * n_chunks]
    features_ref, weight_ref, input_grad_ref, kept_ref, sent_ref, spread, term = refs[2 * n_chunks :]
    at = 0
    for keep, recv in zip(keeps, recvs):
        width = keep.shape[1]
        spread[:, at : at + width] = (keep[...].astype(F32) + recv[...].astype(F32)).astype(BF16)
        at += width
    total = spread[...]
    term[...] = lax.dot_general(features_ref[...], total, (((0,), (0,)), ((), ())), preferred_element_type=F32)
    core, me_gc = lax.axis_index("gr") % 2, lax.axis_index("gc")
    piece = kept_ref.shape[0] // n_gc
    for k in range(n_gc):
        here = pl.multiple_of((core * n_gc + (me_gc ^ k)) * piece, piece)
        there = pl.multiple_of(((1 - core) * n_gc + (me_gc ^ k)) * piece, piece)
        kept_ref[k * piece : (k + 1) * piece] = term[pl.ds(here, piece)]
        sent_ref[k * piece : (k + 1) * piece] = term[pl.ds(there, piece)].astype(BF16)
    input_grad_ref[...] = lax.dot_general(
        total, weight_ref[...], (((1,), (1,)), ((), ())), preferred_element_type=F32
    ).astype(BF16)


def finish(keeps, recvs, features, weight, n_gc):
    n_chunks = len(keeps)
    rows, width = features.shape
    out_width = weight.shape[0]
    return pl.pallas_call(
        functools.partial(finish_kernel, n_gc, n_chunks),
        out_shape=(
            jax.ShapeDtypeStruct((rows, out_width), BF16),
            jax.ShapeDtypeStruct((width // 2, weight.shape[1]), F32),
            jax.ShapeDtypeStruct((width // 2, weight.shape[1]), BF16),
        ),
        in_specs=[VMEM] * (2 * n_chunks + 2),
        out_specs=(VMEM,) * 3,
        scratch_shapes=[
            pltpu.VMEM((rows, weight.shape[1]), BF16),
            pltpu.VMEM((width, weight.shape[1]), F32),
        ],
        compiler_params=params(),
        name="finish",
    )(*keeps, *recvs, features, weight)


def small_call(kernel, outs, args, name):
    return pl.pallas_call(
        kernel,
        out_shape=tuple(jax.ShapeDtypeStruct(s, d) for s, d in outs),
        in_specs=[VMEM] * len(args),
        out_specs=(VMEM,) * len(outs),
        compiler_params=params(16),
        name=name,
    )(*args)


def split_pieces_kernel(n_gc, kept_ref, got_ref, own_ref, *send_refs):
    piece = own_ref.shape[0]
    own_ref[...] = kept_ref[:piece] + got_ref[:piece].astype(F32)
    for k in range(1, n_gc):
        here = slice(k * piece, (k + 1) * piece)
        send_refs[k - 1][...] = (kept_ref[here] + got_ref[here].astype(F32)).astype(BF16)


def plane_sum_kernel(own_ref, *refs):
    total = own_ref[...]
    for ref in refs[:-1]:
        total = total + ref[...].astype(F32)
    refs[-1][...] = total.astype(BF16)


def column_sum_kernel(scale, *refs):
    terms = [ref[...].astype(F32) for ref in refs[:-1]]
    while len(terms) > 1:
        terms = [terms[i] + terms[i + 1] for i in range(0, len(terms), 2)]
    refs[-1][...] = (terms[0] * scale).astype(BF16)


def join_half_kernel(n_gc, *refs):
    out_ref = refs[-1]
    piece = refs[0].shape[0]
    me_gc = lax.axis_index("gc")
    for k in range(n_gc):
        out_ref[pl.ds(pl.multiple_of((me_gc ^ k) * piece, piece), piece)] = refs[k][...]


def join_kernel(mine_ref, other_ref, out_ref):
    half = mine_ref.shape[0]
    core = lax.axis_index("gr") % 2
    out_ref[pl.ds(pl.multiple_of(core * half, half), half)] = mine_ref[...].astype(F32)
    out_ref[pl.ds(pl.multiple_of((1 - core) * half, half), half)] = other_ref[...].astype(F32)


def reduce_weight(kept, sent, n_gr, n_gc, scale):
    half, width = kept.shape
    piece = half // n_gc
    got = xor_permute(sent, "gr", 1)
    own, *sends = small_call(
        functools.partial(split_pieces_kernel, n_gc),
        [((piece, width), F32)] + [((piece, width), BF16)] * (n_gc - 1),
        (kept, got),
        "split_pieces",
    )
    got = [xor_permute(sends[k - 1], "gc", k) for k in range(1, n_gc)]
    (plane,) = small_call(plane_sum_kernel, [((piece, width), BF16)], (own, *got), "plane_sum")
    terms = [plane] + [xor_permute(plane, "gr", 2 * k) for k in range(1, n_gr // 2)]
    (mine,) = small_call(
        functools.partial(column_sum_kernel, scale), [((piece, width), BF16)], terms, "column_sum"
    )
    pieces = [mine] + [xor_permute(mine, "gc", k) for k in range(1, n_gc)]
    (joined,) = small_call(
        functools.partial(join_half_kernel, n_gc), [((half, width), BF16)], pieces, "join_half"
    )
    other = xor_permute(joined, "gr", 1)
    (result,) = small_call(join_kernel, [((2 * half, width), F32)], (joined, other), "join")
    return result


CHUNKS = 4


def local(
    out_grad, preactivation_state, features, weight, block_values, block_rows, block_cols, block_counts
):
    n_gr, n_gc = lax.axis_size("gr"), lax.axis_size("gc")
    node_rows, width = out_grad.shape
    block = block_values.shape[-1]
    columns = node_rows * n_gr // block
    per_part = node_rows // block
    step = width // CHUNKS
    slices = [slice(j * step, (j + 1) * step) for j in range(CHUNKS)]
    gathered = []
    for at in slices:
        grad = out_grad[:, at]
        masked = jnp.where(preactivation_state[:, at] > 0, grad, jnp.zeros_like(grad))
        gathered.append([masked] + [xor_permute(masked, "gc", k) for k in range(1, n_gc)])
    packed = pack(
        block_values[0, 0], block_rows[0, 0], block_cols[0, 0], block_counts[0], n_gr, columns, per_part
    )
    keeps, recvs = [], []
    for parts in gathered:
        keep, send = spmm(packed, parts, columns * block)
        recv = xor_permute(send, "gr", 1)
        mask = 2
        while mask < n_gr:
            total = (keep.astype(F32) + recv.astype(F32)).astype(BF16)
            half = total.shape[0] // 2
            keep = total[:half]
            recv = xor_permute(total[half:], "gr", mask)
            mask *= 2
        keeps.append(keep)
        recvs.append(recv)
    input_grad, kept, sent = finish(keeps, recvs, features, weight, n_gc)
    scale = float((node_rows * n_gr * n_gc) ** -0.5)
    return input_grad, reduce_weight(kept, sent, n_gr, n_gc, scale)


def solution(mesh):
    in_specs = (
        P(("gr", "gc"), None),
        P(("gr", "gc"), None),
        P(("gc", "gr"), None),
        P(),
        P("gr", "gc", None, None, None),
        P("gr", "gc", None),
        P("gr", "gc", None),
        P("gr", "gc"),
    )
    out_specs = (P(("gc", "gr"), None), P())
    return jax.shard_map(local, mesh=mesh, in_specs=in_specs, out_specs=out_specs, check_vma=False)
```

```python
import functools

import jax
import jax.numpy as jnp
from jax import lax
from jax.experimental import pallas as pl
from jax.experimental.pallas import tpu as pltpu
from jax.sharding import PartitionSpec as P

QUAD = 4
UNROLL = 4
GROUPS = ((128, 128, 128, 128),)
TURN_AT = 1
LAST_EARLY = True
SORT_MIB = 16
MASK_MIB = 60
GATHER_AHEAD = False
CORE_LAG = 2
PAIR_LAG = 0
SORT_BYTES = 20_000_000
VMEM = pl.BlockSpec(memory_space=pltpu.VMEM)
SMEM = pl.BlockSpec(memory_space=pltpu.SMEM)
ANY = pl.BlockSpec(memory_space=pl.ANY)
F32 = jnp.float32
BF16 = jnp.bfloat16


def params(mib=48):
    return pltpu.CompilerParams(vmem_limit_bytes=mib * 2**20)


def xor_permute(array, axis, mask):
    size = lax.axis_size(axis)
    return lax.ppermute(array, axis, [(i, i ^ mask) for i in range(size)])


def bit_reversed(index, bits):
    result = 0
    for bit in range(bits):
        result = result + ((index >> bit) & 1) * (1 << (bits - 1 - bit))
    return result


def sort_kernel(
    sizes, rows_ref, cols_ref, count_ref, values_hbm, slot_at_ref, row_at_ref, col_at_ref, groups_ref,
    values_ref, place, sem
):
    staged = pltpu.make_async_copy(values_hbm, values_ref, sem)
    staged.start()
    n_gr, row_blocks, columns, per_part, bits = sizes
    me_gr, me_gc = lax.axis_index("gr"), lax.axis_index("gc")
    count = count_ref[0]

    def row_place(row):
        return ((row // per_part) ^ me_gc) * per_part + row % per_part

    def col_place(col):
        return bit_reversed((col // per_part) ^ me_gr, bits) * per_part + col % per_part

    def clear(c, carry):
        place[c] = 0
        return carry

    lax.fori_loop(0, columns, clear, 0, unroll=4)

    def tally(s, carry):
        c = cols_ref[s]
        place[c] = place[c] + 1
        return carry

    lax.fori_loop(0, count, tally, 0)

    def open_column(c, group):
        held = place[c]
        taken = (held + QUAD - 1) // QUAD
        place[c] = group * QUAD
        home = col_place(c)

        def label(g, carry):
            col_at_ref[g] = home
            for j in range(QUAD):
                slot_at_ref[g * QUAD + j] = 0
                row_at_ref[g * QUAD + j] = row_blocks
            return carry

        lax.fori_loop(group, group + taken, label, 0)
        return group + taken

    total = lax.fori_loop(0, columns, open_column, 0)
    groups_ref[0] = total
    for extra in range(UNROLL):
        col_at_ref[total + extra] = columns
        for j in range(QUAD):
            slot_at_ref[(total + extra) * QUAD + j] = 0
            row_at_ref[(total + extra) * QUAD + j] = row_blocks

    def insert(s, carry):
        c = cols_ref[s]
        at = place[c]
        place[c] = at + 1
        slot_at_ref[at] = s
        row_at_ref[at] = row_place(rows_ref[s])
        return carry

    lax.fori_loop(0, count, insert, 0)
    staged.wait()


def sort_blocks(rows, cols, count, values, n_gr, n_gc, per_part):
    capacity = rows.shape[0]
    columns, row_blocks = n_gr * per_part, n_gc * per_part
    bits = n_gr.bit_length() - 1
    room = (capacity + columns * (QUAD - 1)) // QUAD + UNROLL
    sizes = (n_gr, row_blocks, columns, per_part, bits)
    return pl.pallas_call(
        functools.partial(sort_kernel, sizes),
        out_shape=(
            jax.ShapeDtypeStruct((room * QUAD,), jnp.int32),
            jax.ShapeDtypeStruct((room * QUAD,), jnp.int32),
            jax.ShapeDtypeStruct((room,), jnp.int32),
            jax.ShapeDtypeStruct((1,), jnp.int32),
            jax.ShapeDtypeStruct(values.shape, BF16),
        ),
        in_specs=[SMEM, SMEM, SMEM, ANY],
        out_specs=(SMEM, SMEM, SMEM, SMEM, VMEM),
        scratch_shapes=[pltpu.SMEM((columns,), jnp.int32), pltpu.SemaphoreType.DMA],
        compiler_params=params(SORT_MIB),
        cost_estimate=pl.CostEstimate(flops=0, bytes_accessed=SORT_BYTES, transcendentals=0),
        name="sort_blocks",
    )(rows, cols, count, values)


def mask_kernel(grad_hbm, state_hbm, *refs):
    out_refs, (grad, state, sems) = refs[:-3], refs[-3:]
    copies = [
        pltpu.make_async_copy(grad_hbm, grad, sems.at[0]),
        pltpu.make_async_copy(state_hbm, state, sems.at[1]),
    ]
    for copy in copies:
        copy.start()
    for copy in copies:
        copy.wait()
    masked = jnp.where(state[...] > 0, grad[...], jnp.zeros_like(grad))
    at = 0
    for out_ref in out_refs:
        blocks, width, block = out_ref.shape
        for b in range(blocks):
            out_ref[b] = masked[b * block : (b + 1) * block, at : at + width].T
        at += width


def mask_rows(out_grad, state, block, widths):
    blocks = out_grad.shape[0] // block
    return pl.pallas_call(
        mask_kernel,
        out_shape=tuple(jax.ShapeDtypeStruct((blocks, width, block), BF16) for width in widths),
        in_specs=[ANY, ANY],
        out_specs=(VMEM,) * len(widths),
        scratch_shapes=[
            pltpu.VMEM(out_grad.shape, BF16),
            pltpu.VMEM(out_grad.shape, BF16),
            pltpu.SemaphoreType.DMA((2,)),
        ],
        compiler_params=params(MASK_MIB),
        name="mask_rows",
    )(out_grad, state)


def turn_kernel(own_ref, other_ref, out_ref):
    rows = own_ref.shape[0]
    out_ref[:, :rows] = own_ref[...].T
    out_ref[:, rows:] = other_ref[...].T


def turn_features(own, other):
    rows, width = own.shape
    (result,) = small_call(turn_kernel, [((width, 2 * rows), BF16)], (own, other), "turn_features")
    return result


def weight_kernel(n_gc, n_chunks, *refs):
    keeps, recvs, (last_ref, turned_ref, kept_ref, sent_ref, term) = (
        refs[: n_chunks - 1], refs[n_chunks - 1 : 2 * n_chunks - 2], refs[2 * n_chunks - 2 :]
    )
    at = 0
    for j in range(n_chunks):
        if j + 1 < n_chunks:
            tiles = [
                (keeps[j][b].astype(F32) + recvs[j][b].astype(F32)).astype(BF16)
                for b in range(keeps[j].shape[0])
            ]
        else:
            tiles = [last_ref[b] for b in range(last_ref.shape[0])]
        right = jnp.concatenate(tiles, axis=1)
        width, nodes = right.shape
        term[:, at : at + width] = lax.dot_general(
            turned_ref[:, :nodes], right, (((1,), (1,)), ((), ())), preferred_element_type=F32
        )
        at += width
    core, me_gc = lax.axis_index("gr") % 2, lax.axis_index("gc")
    piece = kept_ref.shape[0] // n_gc
    for k in range(n_gc):
        here = pl.multiple_of((core * n_gc + (me_gc ^ k)) * piece, piece)
        there = pl.multiple_of(((1 - core) * n_gc + (me_gc ^ k)) * piece, piece)
        kept_ref[k * piece : (k + 1) * piece] = term[pl.ds(here, piece)]
        sent_ref[k * piece : (k + 1) * piece] = term[pl.ds(there, piece)].astype(BF16)


def weight_terms(keeps, recvs, last, turned, n_gc):
    sums = (*keeps, last)
    width = turned.shape[0]
    out_width = sum(s.shape[1] for s in sums)
    return pl.pallas_call(
        functools.partial(weight_kernel, n_gc, len(sums)),
        out_shape=(
            jax.ShapeDtypeStruct((width // 2, out_width), F32),
            jax.ShapeDtypeStruct((width // 2, out_width), BF16),
        ),
        in_specs=[VMEM] * (2 * len(sums)),
        out_specs=(VMEM,) * 2,
        scratch_shapes=[pltpu.VMEM((width, out_width), F32)],
        compiler_params=params(16),
        name="weight_terms",
    )(*keeps, *recvs, last, turned)


def spmm_kernel(n_gc, start, slot_at_ref, row_at_ref, col_at_ref, groups_ref, values_ref, *refs):
    parts, (keep_ref, send_ref, stacked, total) = refs[:n_gc], refs[-4:]
    part_blocks = parts[0].shape[0]
    half = keep_ref.shape[0]
    for k in range(n_gc):
        stacked[k * part_blocks : (k + 1) * part_blocks] = parts[k][:, start : start + stacked.shape[1]]
    stacked[n_gc * part_blocks] = jnp.zeros(stacked.shape[1:], BF16)
    total[...] = jnp.zeros_like(total)

    def step(i, carry):
        products = []
        for u in range(UNROLL):
            at = (i * UNROLL + u) * QUAD
            left = jnp.concatenate([stacked[row_at_ref[at + j]] for j in range(QUAD)], axis=1)
            right = jnp.concatenate([values_ref[slot_at_ref[at + j]] for j in range(QUAD)], axis=0)
            products.append(jnp.dot(left, right, preferred_element_type=F32))
        for u in range(UNROLL):
            place = col_at_ref[i * UNROLL + u]
            total[place] = total[place] + products[u]
        return carry

    lax.fori_loop(0, (groups_ref[0] + UNROLL - 1) // UNROLL, step, 0)
    keep_ref[...] = total[:half].astype(BF16)
    send_ref[...] = total[half : 2 * half].astype(BF16)


def spmm(order, parts, start, width, columns, after=()):
    n_gc = len(parts)
    part_blocks, _, block = parts[0].shape
    half = jax.ShapeDtypeStruct((columns // 2, width, block), BF16)
    return pl.pallas_call(
        functools.partial(spmm_kernel, n_gc, start),
        out_shape=(half, half),
        in_specs=[SMEM, SMEM, SMEM, SMEM] + [VMEM] * (n_gc + 1) + [ANY] * len(after),
        out_specs=(VMEM, VMEM),
        scratch_shapes=[
            pltpu.VMEM((n_gc * part_blocks + 1, width, block), BF16),
            pltpu.VMEM((columns + 1, width, block), F32),
        ],
        compiler_params=params(24),
        cost_estimate=pl.CostEstimate(flops=5_000_000_000, bytes_accessed=5_000_000, transcendentals=0),
        name="tile_partial",
    )(*order, *parts, *after)


def finish_kernel(n_chunks, *refs):
    keeps, recvs = refs[:n_chunks], refs[n_chunks : 2 * n_chunks]
    weight_ref, input_grad_ref, spread = refs[2 * n_chunks :]
    at = 0
    for keep, recv in zip(keeps, recvs):
        blocks, width, block = keep.shape
        for b in range(blocks):
            tile = (keep[b].astype(F32) + recv[b].astype(F32)).astype(BF16)
            spread[b * block : (b + 1) * block, at : at + width] = tile.T
        at += width
    input_grad_ref[...] = lax.dot_general(
        spread[...], weight_ref[...], (((1,), (1,)), ((), ())), preferred_element_type=F32
    ).astype(BF16)


def finish(keeps, recvs, weight):
    blocks, _, block = keeps[0].shape
    rows = blocks * block
    return pl.pallas_call(
        functools.partial(finish_kernel, len(keeps)),
        out_shape=jax.ShapeDtypeStruct((rows, weight.shape[0]), BF16),
        in_specs=[VMEM] * (2 * len(keeps) + 1),
        out_specs=VMEM,
        scratch_shapes=[pltpu.VMEM((rows, weight.shape[1]), BF16)],
        compiler_params=params(16),
        name="finish",
    )(*keeps, *recvs, weight)


def small_call(kernel, outs, args, name, after=()):
    return pl.pallas_call(
        kernel,
        out_shape=tuple(jax.ShapeDtypeStruct(s, d) for s, d in outs),
        in_specs=[VMEM] * len(args) + [ANY] * len(after),
        out_specs=(VMEM,) * len(outs),
        compiler_params=params(16),
        name=name,
    )(*args, *after)


def split_pieces_kernel(n_gc, kept_ref, got_ref, own_ref, *send_refs):
    piece = own_ref.shape[0]
    own_ref[...] = kept_ref[:piece] + got_ref[:piece].astype(F32)
    for k in range(1, n_gc):
        here = slice(k * piece, (k + 1) * piece)
        send_refs[k - 1][...] = (kept_ref[here] + got_ref[here].astype(F32)).astype(BF16)


def plane_sum_kernel(terms, own_ref, *refs):
    total = own_ref[...]
    for ref in refs[: terms - 1]:
        total = total + ref[...].astype(F32)
    refs[-1][...] = total.astype(BF16)


def column_sum_kernel(scale, *refs):
    terms = [ref[...].astype(F32) for ref in refs[:-1]]
    while len(terms) > 1:
        terms = [terms[i] + terms[i + 1] for i in range(0, len(terms), 2)]
    refs[-1][...] = (terms[0] * scale).astype(BF16)


def join_half_kernel(n_gc, *refs):
    out_ref = refs[-1]
    piece = refs[0].shape[0]
    me_gc = lax.axis_index("gc")
    for k in range(n_gc):
        out_ref[pl.ds(pl.multiple_of((me_gc ^ k) * piece, piece), piece)] = refs[k][...]


def join_kernel(mine_ref, other_ref, out_ref):
    half = mine_ref.shape[0]
    core = lax.axis_index("gr") % 2
    out_ref[pl.ds(pl.multiple_of(core * half, half), half)] = mine_ref[...].astype(F32)
    out_ref[pl.ds(pl.multiple_of((1 - core) * half, half), half)] = other_ref[...].astype(F32)


def reduce_weight(kept, sent, n_gr, n_gc, scale, after):
    half, width = kept.shape
    piece = half // n_gc
    got = xor_permute(sent, "gr", 1)
    own, *sends = small_call(
        functools.partial(split_pieces_kernel, n_gc),
        [((piece, width), F32)] + [((piece, width), BF16)] * (n_gc - 1),
        (kept, got),
        "split_pieces",
    )
    got = [xor_permute(sends[k - 1], "gc", k) for k in range(1, n_gc)]
    (plane,) = small_call(
        functools.partial(plane_sum_kernel, n_gc), [((piece, width), BF16)], (own, *got), "plane_sum", after
    )
    terms = [plane] + [xor_permute(plane, "gr", 2 * k) for k in range(1, n_gr // 2)]
    (mine,) = small_call(
        functools.partial(column_sum_kernel, scale), [((piece, width), BF16)], terms, "column_sum"
    )
    pieces = [mine] + [xor_permute(mine, "gc", k) for k in range(1, n_gc)]
    (joined,) = small_call(
        functools.partial(join_half_kernel, n_gc), [((half, width), BF16)], pieces, "join_half"
    )
    other = xor_permute(joined, "gr", 1)
    (result,) = small_call(join_kernel, [((2 * half, width), F32)], (joined, other), "join")
    return result


def local(
    out_grad, preactivation_state, features, weight, block_values, block_rows, block_cols, block_counts
):
    n_gr, n_gc = lax.axis_size("gr"), lax.axis_size("gc")
    node_rows, width = out_grad.shape
    block = block_values.shape[-1]
    columns = node_rows * n_gr // block
    per_part = node_rows // block
    masked = mask_rows(out_grad, preactivation_state, block, [sum(group) for group in GROUPS])
    gathered = [[part] + [xor_permute(part, "gc", k) for k in range(1, n_gc)] for part in masked]
    other_features = xor_permute(features, "gr", n_gr // 2)
    order = sort_blocks(
        block_rows[0, 0], block_cols[0, 0], block_counts[0], block_values[0, 0], n_gr, n_gc, per_part
    )
    turned = turn_features(features, other_features)
    chunks = [(g, sum(group[:i]), group[i]) for g, group in enumerate(GROUPS) for i in range(len(group))]
    core_sums, pair_sums, keeps, recvs = [], [], [], []
    for j, (group, start, size) in enumerate(chunks):
        after = []
        if GATHER_AHEAD and j == 0:
            after += [part for parts in gathered[1:] for part in parts[1:]]
        if j == TURN_AT:
            after.append(turned)
        if CORE_LAG and j >= CORE_LAG:
            after.append(core_sums[j - CORE_LAG])
        if PAIR_LAG and j >= PAIR_LAG:
            after.append(pair_sums[j - PAIR_LAG])
        keep, send = spmm(order, gathered[group], start, size, columns, after)
        recv = xor_permute(send, "gr", 1)
        mask = 2
        while mask < n_gr:
            total = (keep.astype(F32) + recv.astype(F32)).astype(BF16)
            if mask == 2:
                core_sums.append(total)
            if 2 * mask == n_gr:
                pair_sums.append(total)
            half = total.shape[0] // 2
            keep = total[:half]
            recv = xor_permute(total[half:], "gr", mask)
            mask *= 2
        keeps.append(keep)
        recvs.append(recv)
    kept, sent = weight_terms(keeps[:-1], recvs[:-1], pair_sums[-1], turned, n_gc)
    scale = float((node_rows * n_gr * n_gc) ** -0.5)
    weight_grad = reduce_weight(kept, sent, n_gr, n_gc, scale, recvs[-1:] if LAST_EARLY else [])
    return finish(keeps, recvs, weight), weight_grad


def solution(mesh):
    in_specs = (
        P(("gr", "gc"), None),
        P(("gr", "gc"), None),
        P(("gc", "gr"), None),
        P(),
        P("gr", "gc", None, None, None),
        P("gr", "gc", None),
        P("gr", "gc", None),
        P("gr", "gc"),
    )
    out_specs = (P(("gc", "gr"), None), P())
    return jax.shard_map(local, mesh=mesh, in_specs=in_specs, out_specs=out_specs, check_vma=False)
```

```python
import functools

import jax
import jax.numpy as jnp
from jax import lax
from jax.experimental import pallas as pl
from jax.experimental.pallas import tpu as pltpu
from jax.sharding import PartitionSpec as P

QUADS = (4, 2)
UNROLL = 4
WIDTHS = (128, 128, 128, 128)
EARLY_MIB = 24
LATE_MIB = 16
TURN_AT = 1
CORE_PIECES = 1
CORE_AFTER = ((), (), (0,), (1,))
PAIR_AFTER = ((), (), (), ())
W_SPREAD = 3
SPLIT_AFTER = 0
PLANE_AFTER = 4
FINISH_LATE = False
SORT_MIB = 16
MASK_MIB = 60
VMEM = pl.BlockSpec(memory_space=pltpu.VMEM)
SMEM = pl.BlockSpec(memory_space=pltpu.SMEM)
ANY = pl.BlockSpec(memory_space=pl.ANY)
F32 = jnp.float32
BF16 = jnp.bfloat16


def params(mib=48):
    return pltpu.CompilerParams(vmem_limit_bytes=mib * 2**20)


def xor_permute(array, axis, mask):
    size = lax.axis_size(axis)
    return lax.ppermute(array, axis, [(i, i ^ mask) for i in range(size)])


def permute_pieces(array, axis, mask, pieces):
    step = array.shape[0] // pieces
    parts = [xor_permute(array[i * step : (i + 1) * step], axis, mask) for i in range(pieces)]
    return parts[0] if pieces == 1 else jnp.concatenate(parts, axis=0)


def bit_reversed(index, bits):
    result = 0
    for bit in range(bits):
        result = result + ((index >> bit) & 1) * (1 << (bits - 1 - bit))
    return result


def layout(capacity, columns):
    places, at = [], 0
    for quad in QUADS:
        room = (capacity + columns * (quad - 1)) // quad + UNROLL
        places.append((quad, at, at + room * quad, at + 2 * room * quad, at + (2 * quad + 1) * room))
        at += (2 * quad + 1) * room + 1
    return places, at


def each_block(count, body):
    def step(i, carry):
        for u in range(4):
            body(i * 4 + u, carry)
        return carry

    whole = count >> 2
    lax.fori_loop(0, whole, step, 0)
    lax.fori_loop(whole * 4, count, body, 0)


def sort_kernel(sizes, rows_ref, cols_ref, count_ref, values_hbm, lists_ref, values_ref, place, sem):
    staged = pltpu.make_async_copy(values_hbm, values_ref, sem)
    staged.start()
    n_gr, n_gc, columns, per_part, capacity, bits = sizes
    shift, within = per_part.bit_length() - 1, per_part - 1
    me_gr, me_gc = lax.axis_index("gr"), lax.axis_index("gc")
    count = count_ref[0]
    (early, late), _ = layout(capacity, columns)

    def fill(start, stop, value):
        def put(i, carry):
            lists_ref[i] = value
            return carry

        lax.fori_loop(start, stop, put, 0, unroll=8)

    for _, slots, rows, cols, total in (early, late):
        fill(slots, rows, 0)
        fill(rows, cols, n_gc * per_part)
        fill(cols, total, columns)

    def clear(c, carry):
        place[c] = 0
        return carry

    lax.fori_loop(0, 2 * columns, clear, 0, unroll=8)

    def cell(s):
        part = (rows_ref[s] >> shift) ^ me_gc
        is_late = part == n_gc - 1
        return part, is_late, jnp.where(is_late, columns, 0) + cols_ref[s]

    def tally(s, carry):
        _, _, c = cell(s)
        place[c] = place[c] + 1
        return carry

    each_block(count, tally)

    for which, (quad, _, _, _, total) in enumerate((early, late)):
        first = which * columns

        def open_column(c, group, first=first, quad=quad):
            held = place[first + c]
            place[first + c] = group * quad
            return group + ((held + quad - 1) >> (quad.bit_length() - 1))

        lists_ref[total] = lax.fori_loop(0, columns, open_column, 0, unroll=4)

    def insert(s, carry):
        part, is_late, c = cell(s)
        at = place[c]
        place[c] = at + 1
        col = cols_ref[s]
        quad, slots, rows, cols = [jnp.where(is_late, late[i], early[i]) for i in range(4)]
        lists_ref[slots + at] = s
        lists_ref[rows + at] = (part << shift) | (rows_ref[s] & within)
        down = jnp.where(is_late, QUADS[1].bit_length() - 1, QUADS[0].bit_length() - 1)
        home = bit_reversed((col >> shift) ^ me_gr, bits)
        lists_ref[cols + (at >> down)] = (home << shift) | (col & within)
        return carry

    each_block(count, insert)
    staged.wait()


def sort_blocks(rows, cols, count, values, n_gr, n_gc, per_part):
    capacity = rows.shape[0]
    columns = n_gr * per_part
    bits = n_gr.bit_length() - 1
    sizes = (n_gr, n_gc, columns, per_part, capacity, bits)
    return pl.pallas_call(
        functools.partial(sort_kernel, sizes),
        out_shape=(
            jax.ShapeDtypeStruct((layout(capacity, columns)[1],), jnp.int32),
            jax.ShapeDtypeStruct(values.shape, BF16),
        ),
        in_specs=[SMEM, SMEM, SMEM, ANY],
        out_specs=(SMEM, VMEM),
        scratch_shapes=[pltpu.SMEM((2 * columns,), jnp.int32), pltpu.SemaphoreType.DMA],
        compiler_params=params(SORT_MIB),
        name="sort_blocks",
    )(rows, cols, count, values)


def mask_kernel(grad_hbm, state_hbm, *refs):
    out_refs, (grad, state, sems) = refs[:-3], refs[-3:]
    copies = [
        pltpu.make_async_copy(grad_hbm, grad, sems.at[0]),
        pltpu.make_async_copy(state_hbm, state, sems.at[1]),
    ]
    for copy in copies:
        copy.start()
    for copy in copies:
        copy.wait()
    masked = jnp.where(state[...] > 0, grad[...], jnp.zeros_like(grad))
    at = 0
    for out_ref in out_refs:
        blocks, width, block = out_ref.shape
        for b in range(blocks):
            out_ref[b] = masked[b * block : (b + 1) * block, at : at + width].T
        at += width


def mask_rows(out_grad, state, block, widths):
    blocks = out_grad.shape[0] // block
    return pl.pallas_call(
        mask_kernel,
        out_shape=tuple(jax.ShapeDtypeStruct((blocks, width, block), BF16) for width in widths),
        in_specs=[ANY, ANY],
        out_specs=(VMEM,) * len(widths),
        scratch_shapes=[
            pltpu.VMEM(out_grad.shape, BF16),
            pltpu.VMEM(out_grad.shape, BF16),
            pltpu.SemaphoreType.DMA((2,)),
        ],
        compiler_params=params(MASK_MIB),
        name="mask_rows",
    )(out_grad, state)


def turn_kernel(own_ref, other_ref, out_ref):
    rows = own_ref.shape[0]
    out_ref[:, :rows] = own_ref[...].T
    out_ref[:, rows:] = other_ref[...].T


def turn_features(own, other):
    rows, width = own.shape
    (result,) = small_call(turn_kernel, [((width, 2 * rows), BF16)], (own, other), "turn_features")
    return result


def weight_kernel(n_gc, n_chunks, *refs):
    lows, others, (turned_ref, kept_ref, sent_ref, term) = (
        refs[:n_chunks], refs[n_chunks : 2 * n_chunks], refs[2 * n_chunks :]
    )
    at = 0
    for j, (low, other) in enumerate(zip(lows, others)):
        blocks = range(low.shape[0])
        if j < W_SPREAD:
            tiles = [(low[b].astype(F32) + other[b].astype(F32)).astype(BF16) for b in blocks]
        else:
            tiles = [ref[b] for ref in (low, other) for b in blocks]
        right = jnp.concatenate(tiles, axis=1)
        width, nodes = right.shape
        term[:, at : at + width] = lax.dot_general(
            turned_ref[:, :nodes], right, (((1,), (1,)), ((), ())), preferred_element_type=F32
        )
        at += width
    core, me_gc = lax.axis_index("gr") % 2, lax.axis_index("gc")
    piece = kept_ref.shape[0] // n_gc
    for k in range(n_gc):
        here = pl.multiple_of((core * n_gc + (me_gc ^ k)) * piece, piece)
        there = pl.multiple_of(((1 - core) * n_gc + (me_gc ^ k)) * piece, piece)
        kept_ref[k * piece : (k + 1) * piece] = term[pl.ds(here, piece)]
        sent_ref[k * piece : (k + 1) * piece] = term[pl.ds(there, piece)].astype(BF16)


def weight_terms(lows, others, turned, n_gc):
    width = turned.shape[0]
    out_width = sum(low.shape[1] for low in lows)
    return pl.pallas_call(
        functools.partial(weight_kernel, n_gc, len(lows)),
        out_shape=(
            jax.ShapeDtypeStruct((width // 2, out_width), F32),
            jax.ShapeDtypeStruct((width // 2, out_width), BF16),
        ),
        in_specs=[VMEM] * (2 * len(lows) + 1),
        out_specs=(VMEM,) * 2,
        scratch_shapes=[pltpu.VMEM((width, out_width), F32)],
        compiler_params=params(16),
        name="weight_terms",
    )(*lows, *others, turned)


def add_products(which, list_ref, values_ref, stacked, total):
    quad, slots_at, rows_at, cols_at, count_at = layout(values_ref.shape[0], total.shape[0] - 1)[0][which]

    def step(i, carry):
        products = []
        for u in range(UNROLL):
            at = (i * UNROLL + u) * quad
            left = jnp.concatenate([stacked[list_ref[rows_at + at + j]] for j in range(quad)], axis=1)
            right = jnp.concatenate([values_ref[list_ref[slots_at + at + j]] for j in range(quad)], axis=0)
            products.append(jnp.dot(left, right, preferred_element_type=F32))
        for u in range(UNROLL):
            place = list_ref[cols_at + i * UNROLL + u]
            total[place] = total[place] + products[u]
        return carry

    lax.fori_loop(0, (list_ref[count_at] + UNROLL - 1) // UNROLL, step, 0)


def early_kernel(n_parts, list_ref, values_ref, *refs):
    parts, (total, stacked) = refs[:n_parts], refs[-2:]
    part_blocks = parts[0].shape[0]
    for k in range(n_parts):
        stacked[k * part_blocks : (k + 1) * part_blocks] = parts[k][...]
    stacked[stacked.shape[0] - 1] = jnp.zeros(stacked.shape[1:], BF16)
    total[...] = jnp.zeros_like(total)
    add_products(0, list_ref, values_ref, stacked, total)


def early_products(blocks, values, parts, n_gc, columns):
    part_blocks, width, block = parts[0].shape
    return pl.pallas_call(
        functools.partial(early_kernel, len(parts)),
        out_shape=jax.ShapeDtypeStruct((columns + 1, width, block), F32),
        in_specs=[SMEM] + [VMEM] * (len(parts) + 1),
        out_specs=VMEM,
        scratch_shapes=[pltpu.VMEM((n_gc * part_blocks + 1, width, block), BF16)],
        compiler_params=params(EARLY_MIB),
        name="early_products",
    )(blocks, values, *parts)


def spmm_kernel(start, list_ref, values_ref, part_ref, early_hbm, *refs):
    keep_ref, send_ref, stacked, total, sem = refs[-5:]
    width = total.shape[1]
    part_blocks = part_ref.shape[0]
    half = keep_ref.shape[0]
    copy = pltpu.make_async_copy(early_hbm.at[:, pl.ds(start, width)], total, sem)
    copy.start()
    last = stacked.shape[0] - 1
    stacked[last - part_blocks : last] = part_ref[:, start : start + width]
    stacked[last] = jnp.zeros(stacked.shape[1:], BF16)
    copy.wait()
    add_products(1, list_ref, values_ref, stacked, total)
    keep_ref[...] = total[:half].astype(BF16)
    send_ref[...] = total[half : 2 * half].astype(BF16)


def spmm(blocks, values, part, early, start, width, n_gc, columns, after=()):
    part_blocks, _, block = part.shape
    half = jax.ShapeDtypeStruct((columns // 2, width, block), BF16)
    return pl.pallas_call(
        functools.partial(spmm_kernel, start),
        out_shape=(half, half),
        in_specs=[SMEM, VMEM, VMEM, ANY] + [ANY] * len(after),
        out_specs=(VMEM, VMEM),
        scratch_shapes=[
            pltpu.VMEM((n_gc * part_blocks + 1, width, block), BF16),
            pltpu.VMEM((columns + 1, width, block), F32),
            pltpu.SemaphoreType.DMA,
        ],
        compiler_params=params(LATE_MIB),
        name="tile_partial",
    )(blocks, values, part, early, *after)


def add_kernel(keep_ref, recv_ref, *refs):
    low_ref, high_ref = refs[-2:]
    half = low_ref.shape[0]
    low_ref[...] = (keep_ref[:half].astype(F32) + recv_ref[:half].astype(F32)).astype(BF16)
    high_ref[...] = (keep_ref[half:].astype(F32) + recv_ref[half:].astype(F32)).astype(BF16)


def add_halves(keep, recv, after):
    half = (keep.shape[0] // 2, *keep.shape[1:])
    return small_call(add_kernel, [(half, BF16)] * 2, (keep, recv), "add_halves", after)


def finish_kernel(n_chunks, *refs):
    keeps, recvs = refs[:n_chunks], refs[n_chunks : 2 * n_chunks]
    weight_ref, input_grad_ref, spread = refs[2 * n_chunks], *refs[-2:]
    at = 0
    for keep, recv in zip(keeps, recvs):
        blocks, width, block = keep.shape
        for b in range(blocks):
            tile = (keep[b].astype(F32) + recv[b].astype(F32)).astype(BF16)
            spread[b * block : (b + 1) * block, at : at + width] = tile.T
        at += width
    input_grad_ref[...] = lax.dot_general(
        spread[...], weight_ref[...], (((1,), (1,)), ((), ())), preferred_element_type=F32
    ).astype(BF16)


def finish(keeps, recvs, weight, after):
    blocks, _, block = keeps[0].shape
    rows = blocks * block
    return pl.pallas_call(
        functools.partial(finish_kernel, len(keeps)),
        out_shape=jax.ShapeDtypeStruct((rows, weight.shape[0]), BF16),
        in_specs=[VMEM] * (2 * len(keeps) + 1) + [ANY] * len(after),
        out_specs=VMEM,
        scratch_shapes=[pltpu.VMEM((rows, weight.shape[1]), BF16)],
        compiler_params=params(16),
        name="finish",
    )(*keeps, *recvs, weight, *after)


def small_call(kernel, outs, args, name, after=()):
    return pl.pallas_call(
        kernel,
        out_shape=tuple(jax.ShapeDtypeStruct(s, d) for s, d in outs),
        in_specs=[VMEM] * len(args) + [ANY] * len(after),
        out_specs=(VMEM,) * len(outs),
        compiler_params=params(16),
        name=name,
    )(*args, *after)


def split_pieces_kernel(n_gc, kept_ref, got_ref, *refs):
    own_ref, *send_refs = refs[-n_gc:]
    piece = own_ref.shape[0]
    own_ref[...] = kept_ref[:piece] + got_ref[:piece].astype(F32)
    for k in range(1, n_gc):
        here = slice(k * piece, (k + 1) * piece)
        send_refs[k - 1][...] = (kept_ref[here] + got_ref[here].astype(F32)).astype(BF16)


def plane_sum_kernel(terms, own_ref, *refs):
    total = own_ref[...]
    for ref in refs[: terms - 1]:
        total = total + ref[...].astype(F32)
    refs[-1][...] = total.astype(BF16)


def column_sum_kernel(count, scale, *refs):
    terms = [ref[...].astype(F32) for ref in refs[:count]]
    while len(terms) > 1:
        terms = [terms[i] + terms[i + 1] for i in range(0, len(terms), 2)]
    refs[-1][...] = (terms[0] * scale).astype(BF16)


def join_half_kernel(n_gc, *refs):
    out_ref = refs[-1]
    piece = refs[0].shape[0]
    me_gc = lax.axis_index("gc")
    for k in range(n_gc):
        out_ref[pl.ds(pl.multiple_of((me_gc ^ k) * piece, piece), piece)] = refs[k][...]


def join_kernel(mine_ref, other_ref, out_ref):
    half = mine_ref.shape[0]
    core = lax.axis_index("gr") % 2
    out_ref[pl.ds(pl.multiple_of(core * half, half), half)] = mine_ref[...].astype(F32)
    out_ref[pl.ds(pl.multiple_of((1 - core) * half, half), half)] = other_ref[...].astype(F32)


def local(
    out_grad, preactivation_state, features, weight, block_values, block_rows, block_cols, block_counts
):
    n_gr, n_gc = lax.axis_size("gr"), lax.axis_size("gc")
    node_rows, width = out_grad.shape
    block = block_values.shape[-1]
    columns = node_rows * n_gr // block
    per_part = node_rows // block
    (masked,) = mask_rows(out_grad, preactivation_state, block, [width])
    parts = [masked] + [xor_permute(masked, "gc", k) for k in range(1, n_gc)]
    other_features = xor_permute(features, "gr", n_gr // 2)
    lists, values = sort_blocks(
        block_rows[0, 0], block_cols[0, 0], block_counts[0], block_values[0, 0], n_gr, n_gc, per_part
    )
    turned = turn_features(features, other_features)
    early = early_products(lists, values, parts[:-1], n_gc, columns)
    core_sums, keeps, recvs, products = [], [], [], []
    for j, size in enumerate(WIDTHS):
        after = [turned] if j == TURN_AT else []
        after += products[-1:] + [core_sums[k] for k in CORE_AFTER[j]]
        keep, send = spmm(lists, values, parts[-1], early, sum(WIDTHS[:j]), size, n_gc, columns, after)
        products.append(keep)
        recv = permute_pieces(send, "gr", 1, CORE_PIECES)
        total = (keep.astype(F32) + recv.astype(F32)).astype(BF16)
        core_sums.append(total)
        keeps.append(total[: columns // 4])
        recvs.append(xor_permute(total[columns // 4 :], "gr", 2))
    lows, highs, lasts = [], [], []
    for j in range(len(WIDTHS)):
        low, recv, mask = keeps[j], recvs[j], 2
        while 2 * mask < n_gr:
            if PAIR_AFTER[j]:
                low, high = add_halves(low, recv, [core_sums[k] for k in PAIR_AFTER[j]])
            else:
                total = (low.astype(F32) + recv.astype(F32)).astype(BF16)
                low, high = total[: total.shape[0] // 2], total[total.shape[0] // 2 :]
            mask *= 2
            recv = xor_permute(high, "gr", mask)
        lows.append(low)
        highs.append(high)
        lasts.append(recv)
    others = [lasts[j] if j < W_SPREAD else highs[j] for j in range(len(WIDTHS))]
    kept, sent = weight_terms(lows, others, turned, n_gc)
    half = width // 2
    piece = half // n_gc
    got = xor_permute(sent, "gr", 1)
    own, *sends = small_call(
        functools.partial(split_pieces_kernel, n_gc),
        [((piece, width), F32)] + [((piece, width), BF16)] * (n_gc - 1),
        (kept, got),
        "split_pieces",
        lasts[W_SPREAD:SPLIT_AFTER],
    )
    got = [xor_permute(sends[k - 1], "gc", k) for k in range(1, n_gc)]
    (plane,) = small_call(
        functools.partial(plane_sum_kernel, n_gc),
        [((piece, width), BF16)],
        (own, *got),
        "plane_sum",
        lasts[max(W_SPREAD, SPLIT_AFTER) : PLANE_AFTER],
    )
    terms = [plane] + [xor_permute(plane, "gr", 2 * k) for k in range(1, n_gr // 2)]
    scale = float((node_rows * n_gr * n_gc) ** -0.5)
    (mine,) = small_call(
        functools.partial(column_sum_kernel, len(terms), scale),
        [((piece, width), BF16)],
        terms,
        "column_sum",
    )
    pieces = [mine] + [xor_permute(mine, "gc", k) for k in range(1, n_gc)]
    input_grad = finish(lows, lasts, weight, [mine] if FINISH_LATE else [])
    (joined,) = small_call(
        functools.partial(join_half_kernel, n_gc),
        [((half, width), BF16)],
        pieces,
        "join_half",
        [input_grad] if FINISH_LATE else [],
    )
    other = xor_permute(joined, "gr", 1)
    (weight_grad,) = small_call(join_kernel, [((width, width), F32)], (joined, other), "join")
    return input_grad, weight_grad


def solution(mesh):
    in_specs = (
        P(("gr", "gc"), None),
        P(("gr", "gc"), None),
        P(("gc", "gr"), None),
        P(),
        P("gr", "gc", None, None, None),
        P("gr", "gc", None),
        P("gr", "gc", None),
        P("gr", "gc"),
    )
    out_specs = (P(("gc", "gr"), None), P())
    return jax.shard_map(local, mesh=mesh, in_specs=in_specs, out_specs=out_specs, check_vma=False)
```

```python
import functools

import jax
import jax.numpy as jnp
from jax import lax
from jax.experimental import pallas as pl
from jax.experimental.pallas import tpu as pltpu
from jax.sharding import PartitionSpec as P

QUADS = (4, 2)
UNROLL = 4
WIDTHS = (128, 128, 128, 128)
EARLY_MIB = 24
LATE_MIB = 16
TURN_AT = 1
CORE_PIECES = 1
CORE_AFTER = ((), (), (0,), (1,))
PAIR_AFTER = ((), (2, 3), (), ())
W_SPREAD = 3
SPLIT_AFTER = 0
PLANE_AFTER = 4
FINISH_LATE = False
SORT_MIB = 16
MASK_MIB = 60
VMEM = pl.BlockSpec(memory_space=pltpu.VMEM)
SMEM = pl.BlockSpec(memory_space=pltpu.SMEM)
ANY = pl.BlockSpec(memory_space=pl.ANY)
F32 = jnp.float32
BF16 = jnp.bfloat16


def params(mib=48):
    return pltpu.CompilerParams(vmem_limit_bytes=mib * 2**20)


def xor_permute(array, axis, mask):
    size = lax.axis_size(axis)
    return lax.ppermute(array, axis, [(i, i ^ mask) for i in range(size)])


def permute_pieces(array, axis, mask, pieces):
    step = array.shape[0] // pieces
    parts = [xor_permute(array[i * step : (i + 1) * step], axis, mask) for i in range(pieces)]
    return parts[0] if pieces == 1 else jnp.concatenate(parts, axis=0)


def bit_reversed(index, bits):
    result = 0
    for bit in range(bits):
        result = result + ((index >> bit) & 1) * (1 << (bits - 1 - bit))
    return result


def layout(capacity, columns):
    places, at = [], 0
    for quad in QUADS:
        room = (capacity + columns * (quad - 1)) // quad + UNROLL
        places.append((quad, at, at + room * quad, at + 2 * room * quad, at + (2 * quad + 1) * room))
        at += (2 * quad + 1) * room + 1
    return places, at


def each_block(count, body):
    def step(i, carry):
        for u in range(4):
            body(i * 4 + u, carry)
        return carry

    whole = count >> 2
    lax.fori_loop(0, whole, step, 0)
    lax.fori_loop(whole * 4, count, body, 0)


def sort_kernel(sizes, rows_ref, cols_ref, count_ref, values_hbm, lists_ref, values_ref, place, sem):
    staged = pltpu.make_async_copy(values_hbm, values_ref, sem)
    staged.start()
    n_gr, n_gc, columns, per_part, capacity, bits = sizes
    shift, within = per_part.bit_length() - 1, per_part - 1
    me_gr, me_gc = lax.axis_index("gr"), lax.axis_index("gc")
    count = count_ref[0]
    (early, late), _ = layout(capacity, columns)

    def fill(start, stop, value):
        def put(i, carry):
            lists_ref[i] = value
            return carry

        lax.fori_loop(start, stop, put, 0, unroll=8)

    for _, slots, rows, cols, total in (early, late):
        fill(slots, rows, 0)
        fill(rows, cols, n_gc * per_part)
        fill(cols, total, columns)

    def clear(c, carry):
        place[c] = 0
        return carry

    lax.fori_loop(0, 2 * columns, clear, 0, unroll=8)

    def cell(s):
        part = (rows_ref[s] >> shift) ^ me_gc
        is_late = part == n_gc - 1
        return part, is_late, jnp.where(is_late, columns, 0) + cols_ref[s]

    def tally(s, carry):
        _, _, c = cell(s)
        place[c] = place[c] + 1
        return carry

    each_block(count, tally)

    for which, (quad, _, _, _, total) in enumerate((early, late)):
        first = which * columns

        def open_column(c, group, first=first, quad=quad):
            held = place[first + c]
            place[first + c] = group * quad
            return group + ((held + quad - 1) >> (quad.bit_length() - 1))

        lists_ref[total] = lax.fori_loop(0, columns, open_column, 0, unroll=4)

    def insert(s, carry):
        part, is_late, c = cell(s)
        at = place[c]
        place[c] = at + 1
        col = cols_ref[s]
        quad, slots, rows, cols = [jnp.where(is_late, late[i], early[i]) for i in range(4)]
        lists_ref[slots + at] = s
        lists_ref[rows + at] = (part << shift) | (rows_ref[s] & within)
        down = jnp.where(is_late, QUADS[1].bit_length() - 1, QUADS[0].bit_length() - 1)
        home = bit_reversed((col >> shift) ^ me_gr, bits)
        lists_ref[cols + (at >> down)] = (home << shift) | (col & within)
        return carry

    each_block(count, insert)
    staged.wait()


def sort_blocks(rows, cols, count, values, n_gr, n_gc, per_part):
    capacity = rows.shape[0]
    columns = n_gr * per_part
    bits = n_gr.bit_length() - 1
    sizes = (n_gr, n_gc, columns, per_part, capacity, bits)
    return pl.pallas_call(
        functools.partial(sort_kernel, sizes),
        out_shape=(
            jax.ShapeDtypeStruct((layout(capacity, columns)[1],), jnp.int32),
            jax.ShapeDtypeStruct(values.shape, BF16),
        ),
        in_specs=[SMEM, SMEM, SMEM, ANY],
        out_specs=(SMEM, VMEM),
        scratch_shapes=[pltpu.SMEM((2 * columns,), jnp.int32), pltpu.SemaphoreType.DMA],
        compiler_params=params(SORT_MIB),
        name="sort_blocks",
    )(rows, cols, count, values)


def mask_kernel(grad_hbm, state_hbm, *refs):
    out_refs, (grad, state, sems) = refs[:-3], refs[-3:]
    copies = [
        pltpu.make_async_copy(grad_hbm, grad, sems.at[0]),
        pltpu.make_async_copy(state_hbm, state, sems.at[1]),
    ]
    for copy in copies:
        copy.start()
    for copy in copies:
        copy.wait()
    masked = jnp.where(state[...] > 0, grad[...], jnp.zeros_like(grad))
    at = 0
    for out_ref in out_refs:
        blocks, width, block = out_ref.shape
        for b in range(blocks):
            out_ref[b] = masked[b * block : (b + 1) * block, at : at + width].T
        at += width


def mask_rows(out_grad, state, block, widths):
    blocks = out_grad.shape[0] // block
    return pl.pallas_call(
        mask_kernel,
        out_shape=tuple(jax.ShapeDtypeStruct((blocks, width, block), BF16) for width in widths),
        in_specs=[ANY, ANY],
        out_specs=(VMEM,) * len(widths),
        scratch_shapes=[
            pltpu.VMEM(out_grad.shape, BF16),
            pltpu.VMEM(out_grad.shape, BF16),
            pltpu.SemaphoreType.DMA((2,)),
        ],
        compiler_params=params(MASK_MIB),
        name="mask_rows",
    )(out_grad, state)


def turn_kernel(own_ref, other_ref, out_ref):
    rows = own_ref.shape[0]
    out_ref[:, :rows] = own_ref[...].T
    out_ref[:, rows:] = other_ref[...].T


def turn_features(own, other):
    rows, width = own.shape
    (result,) = small_call(turn_kernel, [((width, 2 * rows), BF16)], (own, other), "turn_features")
    return result


def weight_kernel(n_gc, n_chunks, *refs):
    lows, others, (turned_ref, kept_ref, sent_ref, term) = (
        refs[:n_chunks], refs[n_chunks : 2 * n_chunks], refs[2 * n_chunks :]
    )
    at = 0
    for j, (low, other) in enumerate(zip(lows, others)):
        blocks = range(low.shape[0])
        if j < W_SPREAD:
            tiles = [(low[b].astype(F32) + other[b].astype(F32)).astype(BF16) for b in blocks]
        else:
            tiles = [ref[b] for ref in (low, other) for b in blocks]
        right = jnp.concatenate(tiles, axis=1)
        width, nodes = right.shape
        term[:, at : at + width] = lax.dot_general(
            turned_ref[:, :nodes], right, (((1,), (1,)), ((), ())), preferred_element_type=F32
        )
        at += width
    core, me_gc = lax.axis_index("gr") % 2, lax.axis_index("gc")
    piece = kept_ref.shape[0] // n_gc
    for k in range(n_gc):
        here = pl.multiple_of((core * n_gc + (me_gc ^ k)) * piece, piece)
        there = pl.multiple_of(((1 - core) * n_gc + (me_gc ^ k)) * piece, piece)
        kept_ref[k * piece : (k + 1) * piece] = term[pl.ds(here, piece)]
        sent_ref[k * piece : (k + 1) * piece] = term[pl.ds(there, piece)].astype(BF16)


def weight_terms(lows, others, turned, n_gc):
    width = turned.shape[0]
    out_width = sum(low.shape[1] for low in lows)
    return pl.pallas_call(
        functools.partial(weight_kernel, n_gc, len(lows)),
        out_shape=(
            jax.ShapeDtypeStruct((width // 2, out_width), F32),
            jax.ShapeDtypeStruct((width // 2, out_width), BF16),
        ),
        in_specs=[VMEM] * (2 * len(lows) + 1),
        out_specs=(VMEM,) * 2,
        scratch_shapes=[pltpu.VMEM((width, out_width), F32)],
        compiler_params=params(16),
        name="weight_terms",
    )(*lows, *others, turned)


def add_products(which, list_ref, values_ref, stacked, total):
    quad, slots_at, rows_at, cols_at, count_at = layout(values_ref.shape[0], total.shape[0] - 1)[0][which]

    def step(i, carry):
        products = []
        for u in range(UNROLL):
            at = (i * UNROLL + u) * quad
            left = jnp.concatenate([stacked[list_ref[rows_at + at + j]] for j in range(quad)], axis=1)
            right = jnp.concatenate([values_ref[list_ref[slots_at + at + j]] for j in range(quad)], axis=0)
            products.append(jnp.dot(left, right, preferred_element_type=F32))
        for u in range(UNROLL):
            place = list_ref[cols_at + i * UNROLL + u]
            total[place] = total[place] + products[u]
        return carry

    lax.fori_loop(0, (list_ref[count_at] + UNROLL - 1) // UNROLL, step, 0)


def early_kernel(n_parts, list_ref, values_ref, *refs):
    parts, (total, stacked) = refs[:n_parts], refs[-2:]
    part_blocks = parts[0].shape[0]
    for k in range(n_parts):
        stacked[k * part_blocks : (k + 1) * part_blocks] = parts[k][...]
    stacked[stacked.shape[0] - 1] = jnp.zeros(stacked.shape[1:], BF16)
    total[...] = jnp.zeros_like(total)
    add_products(0, list_ref, values_ref, stacked, total)


def early_products(blocks, values, parts, n_gc, columns):
    part_blocks, width, block = parts[0].shape
    return pl.pallas_call(
        functools.partial(early_kernel, len(parts)),
        out_shape=jax.ShapeDtypeStruct((columns + 1, width, block), F32),
        in_specs=[SMEM] + [VMEM] * (len(parts) + 1),
        out_specs=VMEM,
        scratch_shapes=[pltpu.VMEM((n_gc * part_blocks + 1, width, block), BF16)],
        compiler_params=params(EARLY_MIB),
        name="early_products",
    )(blocks, values, *parts)


def spmm_kernel(start, list_ref, values_ref, part_ref, early_hbm, *refs):
    keep_ref, send_ref, stacked, total, sem = refs[-5:]
    width = total.shape[1]
    part_blocks = part_ref.shape[0]
    half = keep_ref.shape[0]
    copy = pltpu.make_async_copy(early_hbm.at[:, pl.ds(start, width)], total, sem)
    copy.start()
    last = stacked.shape[0] - 1
    stacked[last - part_blocks : last] = part_ref[:, start : start + width]
    stacked[last] = jnp.zeros(stacked.shape[1:], BF16)
    copy.wait()
    add_products(1, list_ref, values_ref, stacked, total)
    keep_ref[...] = total[:half].astype(BF16)
    send_ref[...] = total[half : 2 * half].astype(BF16)


def spmm(blocks, values, part, early, start, width, n_gc, columns, after=()):
    part_blocks, _, block = part.shape
    half = jax.ShapeDtypeStruct((columns // 2, width, block), BF16)
    return pl.pallas_call(
        functools.partial(spmm_kernel, start),
        out_shape=(half, half),
        in_specs=[SMEM, VMEM, VMEM, ANY] + [ANY] * len(after),
        out_specs=(VMEM, VMEM),
        scratch_shapes=[
            pltpu.VMEM((n_gc * part_blocks + 1, width, block), BF16),
            pltpu.VMEM((columns + 1, width, block), F32),
            pltpu.SemaphoreType.DMA,
        ],
        compiler_params=params(LATE_MIB),
        name="tile_partial",
    )(blocks, values, part, early, *after)


def add_kernel(keep_ref, recv_ref, *refs):
    low_ref, high_ref = refs[-2:]
    half = low_ref.shape[0]
    low_ref[...] = (keep_ref[:half].astype(F32) + recv_ref[:half].astype(F32)).astype(BF16)
    high_ref[...] = (keep_ref[half:].astype(F32) + recv_ref[half:].astype(F32)).astype(BF16)


def add_halves(keep, recv, after):
    half = (keep.shape[0] // 2, *keep.shape[1:])
    return small_call(add_kernel, [(half, BF16)] * 2, (keep, recv), "add_halves", after)


def finish_kernel(n_chunks, *refs):
    keeps, recvs = refs[:n_chunks], refs[n_chunks : 2 * n_chunks]
    weight_ref, input_grad_ref, spread = refs[2 * n_chunks], *refs[-2:]
    at = 0
    for keep, recv in zip(keeps, recvs):
        blocks, width, block = keep.shape
        for b in range(blocks):
            tile = (keep[b].astype(F32) + recv[b].astype(F32)).astype(BF16)
            spread[b * block : (b + 1) * block, at : at + width] = tile.T
        at += width
    input_grad_ref[...] = lax.dot_general(
        spread[...], weight_ref[...], (((1,), (1,)), ((), ())), preferred_element_type=F32
    ).astype(BF16)


def finish(keeps, recvs, weight, after):
    blocks, _, block = keeps[0].shape
    rows = blocks * block
    return pl.pallas_call(
        functools.partial(finish_kernel, len(keeps)),
        out_shape=jax.ShapeDtypeStruct((rows, weight.shape[0]), BF16),
        in_specs=[VMEM] * (2 * len(keeps) + 1) + [ANY] * len(after),
        out_specs=VMEM,
        scratch_shapes=[pltpu.VMEM((rows, weight.shape[1]), BF16)],
        compiler_params=params(16),
        name="finish",
    )(*keeps, *recvs, weight, *after)


def small_call(kernel, outs, args, name, after=()):
    return pl.pallas_call(
        kernel,
        out_shape=tuple(jax.ShapeDtypeStruct(s, d) for s, d in outs),
        in_specs=[VMEM] * len(args) + [ANY] * len(after),
        out_specs=(VMEM,) * len(outs),
        compiler_params=params(16),
        name=name,
    )(*args, *after)


def split_pieces_kernel(n_gc, kept_ref, got_ref, *refs):
    own_ref, *send_refs = refs[-n_gc:]
    piece = own_ref.shape[0]
    own_ref[...] = kept_ref[:piece] + got_ref[:piece].astype(F32)
    for k in range(1, n_gc):
        here = slice(k * piece, (k + 1) * piece)
        send_refs[k - 1][...] = (kept_ref[here] + got_ref[here].astype(F32)).astype(BF16)


def plane_sum_kernel(terms, own_ref, *refs):
    total = own_ref[...]
    for ref in refs[: terms - 1]:
        total = total + ref[...].astype(F32)
    refs[-1][...] = total.astype(BF16)


def column_sum_kernel(count, scale, *refs):
    terms = [ref[...].astype(F32) for ref in refs[:count]]
    while len(terms) > 1:
        terms = [terms[i] + terms[i + 1] for i in range(0, len(terms), 2)]
    refs[-1][...] = (terms[0] * scale).astype(BF16)


def join_half_kernel(n_gc, *refs):
    out_ref = refs[-1]
    piece = refs[0].shape[0]
    me_gc = lax.axis_index("gc")
    for k in range(n_gc):
        out_ref[pl.ds(pl.multiple_of((me_gc ^ k) * piece, piece), piece)] = refs[k][...]


def join_kernel(mine_ref, other_ref, out_ref):
    half = mine_ref.shape[0]
    core = lax.axis_index("gr") % 2
    out_ref[pl.ds(pl.multiple_of(core * half, half), half)] = mine_ref[...].astype(F32)
    out_ref[pl.ds(pl.multiple_of((1 - core) * half, half), half)] = other_ref[...].astype(F32)


def local(
    out_grad, preactivation_state, features, weight, block_values, block_rows, block_cols, block_counts
):
    n_gr, n_gc = lax.axis_size("gr"), lax.axis_size("gc")
    node_rows, width = out_grad.shape
    block = block_values.shape[-1]
    columns = node_rows * n_gr // block
    per_part = node_rows // block
    (masked,) = mask_rows(out_grad, preactivation_state, block, [width])
    parts = [masked] + [xor_permute(masked, "gc", k) for k in range(1, n_gc)]
    other_features = xor_permute(features, "gr", n_gr // 2)
    lists, values = sort_blocks(
        block_rows[0, 0], block_cols[0, 0], block_counts[0], block_values[0, 0], n_gr, n_gc, per_part
    )
    turned = turn_features(features, other_features)
    early = early_products(lists, values, parts[:-1], n_gc, columns)
    core_sums, keeps, recvs, products = [], [], [], []
    for j, size in enumerate(WIDTHS):
        after = [turned] if j == TURN_AT else []
        after += products[-1:] + [core_sums[k] for k in CORE_AFTER[j]]
        keep, send = spmm(lists, values, parts[-1], early, sum(WIDTHS[:j]), size, n_gc, columns, after)
        products.append(keep)
        recv = permute_pieces(send, "gr", 1, CORE_PIECES)
        total = (keep.astype(F32) + recv.astype(F32)).astype(BF16)
        core_sums.append(total)
        keeps.append(total[: columns // 4])
        recvs.append(xor_permute(total[columns // 4 :], "gr", 2))
    lows, highs, lasts = [], [], []
    for j in range(len(WIDTHS)):
        low, recv, mask = keeps[j], recvs[j], 2
        while 2 * mask < n_gr:
            if PAIR_AFTER[j]:
                low, high = add_halves(low, recv, [core_sums[k] for k in PAIR_AFTER[j]])
            else:
                total = (low.astype(F32) + recv.astype(F32)).astype(BF16)
                low, high = total[: total.shape[0] // 2], total[total.shape[0] // 2 :]
            mask *= 2
            recv = xor_permute(high, "gr", mask)
        lows.append(low)
        highs.append(high)
        lasts.append(recv)
    others = [lasts[j] if j < W_SPREAD else highs[j] for j in range(len(WIDTHS))]
    kept, sent = weight_terms(lows, others, turned, n_gc)
    half = width // 2
    piece = half // n_gc
    got = xor_permute(sent, "gr", 1)
    own, *sends = small_call(
        functools.partial(split_pieces_kernel, n_gc),
        [((piece, width), F32)] + [((piece, width), BF16)] * (n_gc - 1),
        (kept, got),
        "split_pieces",
        lasts[W_SPREAD:SPLIT_AFTER],
    )
    got = [xor_permute(sends[k - 1], "gc", k) for k in range(1, n_gc)]
    (plane,) = small_call(
        functools.partial(plane_sum_kernel, n_gc),
        [((piece, width), BF16)],
        (own, *got),
        "plane_sum",
        lasts[max(W_SPREAD, SPLIT_AFTER) : PLANE_AFTER],
    )
    terms = [plane] + [xor_permute(plane, "gr", 2 * k) for k in range(1, n_gr // 2)]
    scale = float((node_rows * n_gr * n_gc) ** -0.5)
    (mine,) = small_call(
        functools.partial(column_sum_kernel, len(terms), scale),
        [((piece, width), BF16)],
        terms,
        "column_sum",
    )
    pieces = [mine] + [xor_permute(mine, "gc", k) for k in range(1, n_gc)]
    input_grad = finish(lows, lasts, weight, [mine] if FINISH_LATE else [])
    (joined,) = small_call(
        functools.partial(join_half_kernel, n_gc),
        [((half, width), BF16)],
        pieces,
        "join_half",
        [input_grad] if FINISH_LATE else [],
    )
    other = xor_permute(joined, "gr", 1)
    (weight_grad,) = small_call(join_kernel, [((width, width), F32)], (joined, other), "join")
    return input_grad, weight_grad


def solution(mesh):
    in_specs = (
        P(("gr", "gc"), None),
        P(("gr", "gc"), None),
        P(("gc", "gr"), None),
        P(),
        P("gr", "gc", None, None, None),
        P("gr", "gc", None),
        P("gr", "gc", None),
        P("gr", "gc"),
    )
    out_specs = (P(("gc", "gr"), None), P())
    return jax.shard_map(local, mesh=mesh, in_specs=in_specs, out_specs=out_specs, check_vma=False)
```

```python
import functools

import jax
import jax.numpy as jnp
from jax import lax
from jax.experimental import pallas as pl
from jax.experimental.pallas import tpu as pltpu
from jax.sharding import PartitionSpec as P

QUADS = (4, 2)
UNROLL = 6
WIDTHS = (128, 128, 128, 128)
EARLY_MIB = 24
LATE_MIB = 16
TURN_AT = 1
CORE_PIECES = 1
CORE_AFTER = ((), (), (0,), (1,))
PAIR_AFTER = ((), (2, 3), (), ())
W_SPREAD = 3
PART_ORDER = (1, 2, 3)
SPLIT_AFTER = 0
PLANE_AFTER = 4
FINISH_LATE = False
SORT_MIB = 16
MASK_MIB = 60
VMEM = pl.BlockSpec(memory_space=pltpu.VMEM)
SMEM = pl.BlockSpec(memory_space=pltpu.SMEM)
ANY = pl.BlockSpec(memory_space=pl.ANY)
F32 = jnp.float32
BF16 = jnp.bfloat16


def params(mib=48):
    return pltpu.CompilerParams(vmem_limit_bytes=mib * 2**20)


def xor_permute(array, axis, mask):
    size = lax.axis_size(axis)
    return lax.ppermute(array, axis, [(i, i ^ mask) for i in range(size)])


def permute_pieces(array, axis, mask, pieces):
    step = array.shape[0] // pieces
    parts = [xor_permute(array[i * step : (i + 1) * step], axis, mask) for i in range(pieces)]
    return parts[0] if pieces == 1 else jnp.concatenate(parts, axis=0)


def bit_reversed(index, bits):
    result = 0
    for bit in range(bits):
        result = result + ((index >> bit) & 1) * (1 << (bits - 1 - bit))
    return result


def layout(capacity, columns):
    places, at = [], 0
    for quad in QUADS:
        room = (capacity + columns * (quad - 1)) // quad + UNROLL
        places.append((quad, at, at + room * quad, at + 2 * room * quad, at + (2 * quad + 1) * room))
        at += (2 * quad + 1) * room + 1
    return places, at


def each_block(count, body):
    def step(i, carry):
        for u in range(4):
            body(i * 4 + u, carry)
        return carry

    whole = count >> 2
    lax.fori_loop(0, whole, step, 0)
    lax.fori_loop(whole * 4, count, body, 0)


def sort_kernel(sizes, rows_ref, cols_ref, count_ref, values_hbm, lists_ref, values_ref, place, sem):
    staged = pltpu.make_async_copy(values_hbm, values_ref, sem)
    staged.start()
    n_gr, n_gc, columns, per_part, capacity, bits = sizes
    shift, within = per_part.bit_length() - 1, per_part - 1
    me_gr, me_gc = lax.axis_index("gr"), lax.axis_index("gc")
    count = count_ref[0]
    (early, late), _ = layout(capacity, columns)

    def fill(start, stop, value):
        def put(i, carry):
            lists_ref[i] = value
            return carry

        lax.fori_loop(start, stop, put, 0, unroll=8)

    for _, slots, rows, cols, total in (early, late):
        fill(slots, rows, 0)
        fill(rows, cols, n_gc * per_part)
        fill(cols, total, columns)

    def clear(c, carry):
        place[c] = 0
        return carry

    lax.fori_loop(0, 2 * columns, clear, 0, unroll=8)

    def cell(s):
        part = (rows_ref[s] >> shift) ^ me_gc
        is_late = part == n_gc - 1
        return part, is_late, jnp.where(is_late, columns, 0) + cols_ref[s]

    def tally(s, carry):
        _, _, c = cell(s)
        place[c] = place[c] + 1
        return carry

    each_block(count, tally)

    for which, (quad, _, _, _, total) in enumerate((early, late)):
        first = which * columns

        def open_column(c, group, first=first, quad=quad):
            held = place[first + c]
            place[first + c] = group * quad
            return group + ((held + quad - 1) >> (quad.bit_length() - 1))

        lists_ref[total] = lax.fori_loop(0, columns, open_column, 0, unroll=4)

    def insert(s, carry):
        part, is_late, c = cell(s)
        at = place[c]
        place[c] = at + 1
        col = cols_ref[s]
        quad, slots, rows, cols = [jnp.where(is_late, late[i], early[i]) for i in range(4)]
        lists_ref[slots + at] = s
        lists_ref[rows + at] = (part << shift) | (rows_ref[s] & within)
        down = jnp.where(is_late, QUADS[1].bit_length() - 1, QUADS[0].bit_length() - 1)
        home = bit_reversed((col >> shift) ^ me_gr, bits)
        lists_ref[cols + (at >> down)] = (home << shift) | (col & within)
        return carry

    each_block(count, insert)
    staged.wait()


def sort_blocks(rows, cols, count, values, n_gr, n_gc, per_part):
    capacity = rows.shape[0]
    columns = n_gr * per_part
    bits = n_gr.bit_length() - 1
    sizes = (n_gr, n_gc, columns, per_part, capacity, bits)
    return pl.pallas_call(
        functools.partial(sort_kernel, sizes),
        out_shape=(
            jax.ShapeDtypeStruct((layout(capacity, columns)[1],), jnp.int32),
            jax.ShapeDtypeStruct(values.shape, BF16),
        ),
        in_specs=[SMEM, SMEM, SMEM, ANY],
        out_specs=(SMEM, VMEM),
        scratch_shapes=[pltpu.SMEM((2 * columns,), jnp.int32), pltpu.SemaphoreType.DMA],
        compiler_params=params(SORT_MIB),
        name="sort_blocks",
    )(rows, cols, count, values)


def mask_kernel(grad_hbm, state_hbm, *refs):
    out_refs, (grad, state, sems) = refs[:-3], refs[-3:]
    blocks, _, block = out_refs[0].shape
    copies = []
    for b in range(blocks):
        rows = pl.ds(b * block, block)
        copies.append(
            [
                pltpu.make_async_copy(grad_hbm.at[rows], grad.at[rows], sems.at[0, b]),
                pltpu.make_async_copy(state_hbm.at[rows], state.at[rows], sems.at[1, b]),
            ]
        )
    for pair in copies:
        for copy in pair:
            copy.start()
    for b in range(blocks):
        for copy in copies[b]:
            copy.wait()
        held = grad[b * block : (b + 1) * block]
        masked = jnp.where(state[b * block : (b + 1) * block] > 0, held, jnp.zeros_like(held))
        at = 0
        for out_ref in out_refs:
            width = out_ref.shape[1]
            out_ref[b] = masked[:, at : at + width].T
            at += width


def mask_rows(out_grad, state, block, widths):
    blocks = out_grad.shape[0] // block
    return pl.pallas_call(
        mask_kernel,
        out_shape=tuple(jax.ShapeDtypeStruct((blocks, width, block), BF16) for width in widths),
        in_specs=[ANY, ANY],
        out_specs=(VMEM,) * len(widths),
        scratch_shapes=[
            pltpu.VMEM(out_grad.shape, BF16),
            pltpu.VMEM(out_grad.shape, BF16),
            pltpu.SemaphoreType.DMA((2, blocks)),
        ],
        compiler_params=params(MASK_MIB),
        name="mask_rows",
    )(out_grad, state)


def turn_kernel(own_ref, other_ref, out_ref):
    rows = own_ref.shape[0]
    out_ref[:, :rows] = own_ref[...].T
    out_ref[:, rows:] = other_ref[...].T


def turn_features(own, other):
    rows, width = own.shape
    (result,) = small_call(turn_kernel, [((width, 2 * rows), BF16)], (own, other), "turn_features")
    return result


def weight_kernel(n_gc, n_chunks, *refs):
    lows, others, (turned_ref, kept_ref, sent_ref, term) = (
        refs[:n_chunks], refs[n_chunks : 2 * n_chunks], refs[2 * n_chunks :]
    )
    at = 0
    for j, (low, other) in enumerate(zip(lows, others)):
        blocks = range(low.shape[0])
        if j < W_SPREAD:
            tiles = [(low[b].astype(F32) + other[b].astype(F32)).astype(BF16) for b in blocks]
        else:
            tiles = [ref[b] for ref in (low, other) for b in blocks]
        right = jnp.concatenate(tiles, axis=1)
        width, nodes = right.shape
        term[:, at : at + width] = lax.dot_general(
            turned_ref[:, :nodes], right, (((1,), (1,)), ((), ())), preferred_element_type=F32
        )
        at += width
    core, me_gc = lax.axis_index("gr") % 2, lax.axis_index("gc")
    piece = kept_ref.shape[0] // n_gc
    for k in range(n_gc):
        here = pl.multiple_of((core * n_gc + (me_gc ^ k)) * piece, piece)
        there = pl.multiple_of(((1 - core) * n_gc + (me_gc ^ k)) * piece, piece)
        kept_ref[k * piece : (k + 1) * piece] = term[pl.ds(here, piece)]
        sent_ref[k * piece : (k + 1) * piece] = term[pl.ds(there, piece)].astype(BF16)


def weight_terms(lows, others, turned, n_gc):
    width = turned.shape[0]
    out_width = sum(low.shape[1] for low in lows)
    return pl.pallas_call(
        functools.partial(weight_kernel, n_gc, len(lows)),
        out_shape=(
            jax.ShapeDtypeStruct((width // 2, out_width), F32),
            jax.ShapeDtypeStruct((width // 2, out_width), BF16),
        ),
        in_specs=[VMEM] * (2 * len(lows) + 1),
        out_specs=(VMEM,) * 2,
        scratch_shapes=[pltpu.VMEM((width, out_width), F32)],
        compiler_params=params(16),
        name="weight_terms",
    )(*lows, *others, turned)


def add_products(which, list_ref, values_ref, stacked, total):
    quad, slots_at, rows_at, cols_at, count_at = layout(values_ref.shape[0], total.shape[0] - 1)[0][which]

    def step(i, carry):
        products = []
        for u in range(UNROLL):
            at = (i * UNROLL + u) * quad
            left = jnp.concatenate([stacked[list_ref[rows_at + at + j]] for j in range(quad)], axis=1)
            right = jnp.concatenate([values_ref[list_ref[slots_at + at + j]] for j in range(quad)], axis=0)
            products.append(jnp.dot(left, right, preferred_element_type=F32))
        for u in range(UNROLL):
            place = list_ref[cols_at + i * UNROLL + u]
            total[place] = total[place] + products[u]
        return carry

    lax.fori_loop(0, (list_ref[count_at] + UNROLL - 1) // UNROLL, step, 0)


def early_kernel(turns, list_ref, values_ref, *refs):
    parts, (total, stacked) = refs[: len(turns)], refs[-2:]
    part_blocks = parts[0].shape[0]
    for k, part in zip(turns, parts):
        stacked[k * part_blocks : (k + 1) * part_blocks] = part[...]
    stacked[stacked.shape[0] - 1] = jnp.zeros(stacked.shape[1:], BF16)
    total[...] = jnp.zeros_like(total)
    add_products(0, list_ref, values_ref, stacked, total)


def early_products(blocks, values, parts, turns, n_gc, columns):
    part_blocks, width, block = parts[0].shape
    return pl.pallas_call(
        functools.partial(early_kernel, turns),
        out_shape=jax.ShapeDtypeStruct((columns + 1, width, block), F32),
        in_specs=[SMEM] + [VMEM] * (len(parts) + 1),
        out_specs=VMEM,
        scratch_shapes=[pltpu.VMEM((n_gc * part_blocks + 1, width, block), BF16)],
        compiler_params=params(EARLY_MIB),
        name="early_products",
    )(blocks, values, *parts)


def spmm_kernel(start, list_ref, values_ref, part_ref, early_hbm, *refs):
    keep_ref, send_ref, stacked, total, sem = refs[-5:]
    width = total.shape[1]
    part_blocks = part_ref.shape[0]
    half = keep_ref.shape[0]
    copy = pltpu.make_async_copy(early_hbm.at[:, pl.ds(start, width)], total, sem)
    copy.start()
    last = stacked.shape[0] - 1
    stacked[last - part_blocks : last] = part_ref[:, start : start + width]
    stacked[last] = jnp.zeros(stacked.shape[1:], BF16)
    copy.wait()
    add_products(1, list_ref, values_ref, stacked, total)
    keep_ref[...] = total[:half].astype(BF16)
    send_ref[...] = total[half : 2 * half].astype(BF16)


def spmm(blocks, values, part, early, start, width, n_gc, columns, after=()):
    part_blocks, _, block = part.shape
    half = jax.ShapeDtypeStruct((columns // 2, width, block), BF16)
    return pl.pallas_call(
        functools.partial(spmm_kernel, start),
        out_shape=(half, half),
        in_specs=[SMEM, VMEM, VMEM, ANY] + [ANY] * len(after),
        out_specs=(VMEM, VMEM),
        scratch_shapes=[
            pltpu.VMEM((n_gc * part_blocks + 1, width, block), BF16),
            pltpu.VMEM((columns + 1, width, block), F32),
            pltpu.SemaphoreType.DMA,
        ],
        compiler_params=params(LATE_MIB),
        name="tile_partial",
    )(blocks, values, part, early, *after)


def add_kernel(keep_ref, recv_ref, *refs):
    low_ref, high_ref = refs[-2:]
    half = low_ref.shape[0]
    low_ref[...] = (keep_ref[:half].astype(F32) + recv_ref[:half].astype(F32)).astype(BF16)
    high_ref[...] = (keep_ref[half:].astype(F32) + recv_ref[half:].astype(F32)).astype(BF16)


def add_halves(keep, recv, after):
    half = (keep.shape[0] // 2, *keep.shape[1:])
    return small_call(add_kernel, [(half, BF16)] * 2, (keep, recv), "add_halves", after)


def finish_kernel(n_chunks, *refs):
    keeps, recvs = refs[:n_chunks], refs[n_chunks : 2 * n_chunks]
    weight_ref, input_grad_ref, spread = refs[2 * n_chunks], *refs[-2:]
    at = 0
    for keep, recv in zip(keeps, recvs):
        blocks, width, block = keep.shape
        for b in range(blocks):
            tile = (keep[b].astype(F32) + recv[b].astype(F32)).astype(BF16)
            spread[b * block : (b + 1) * block, at : at + width] = tile.T
        at += width
    input_grad_ref[...] = lax.dot_general(
        spread[...], weight_ref[...], (((1,), (1,)), ((), ())), preferred_element_type=F32
    ).astype(BF16)


def finish(keeps, recvs, weight, after):
    blocks, _, block = keeps[0].shape
    rows = blocks * block
    return pl.pallas_call(
        functools.partial(finish_kernel, len(keeps)),
        out_shape=jax.ShapeDtypeStruct((rows, weight.shape[0]), BF16),
        in_specs=[VMEM] * (2 * len(keeps) + 1) + [ANY] * len(after),
        out_specs=VMEM,
        scratch_shapes=[pltpu.VMEM((rows, weight.shape[1]), BF16)],
        compiler_params=params(16),
        name="finish",
    )(*keeps, *recvs, weight, *after)


def small_call(kernel, outs, args, name, after=()):
    return pl.pallas_call(
        kernel,
        out_shape=tuple(jax.ShapeDtypeStruct(s, d) for s, d in outs),
        in_specs=[VMEM] * len(args) + [ANY] * len(after),
        out_specs=(VMEM,) * len(outs),
        compiler_params=params(16),
        name=name,
    )(*args, *after)


def split_pieces_kernel(n_gc, kept_ref, got_ref, *refs):
    own_ref, *send_refs = refs[-n_gc:]
    piece = own_ref.shape[0]
    own_ref[...] = kept_ref[:piece] + got_ref[:piece].astype(F32)
    for k in range(1, n_gc):
        here = slice(k * piece, (k + 1) * piece)
        send_refs[k - 1][...] = (kept_ref[here] + got_ref[here].astype(F32)).astype(BF16)


def plane_sum_kernel(terms, own_ref, *refs):
    total = own_ref[...]
    for ref in refs[: terms - 1]:
        total = total + ref[...].astype(F32)
    refs[-1][...] = total.astype(BF16)


def column_sum_kernel(count, scale, *refs):
    terms = [ref[...].astype(F32) for ref in refs[:count]]
    while len(terms) > 1:
        terms = [terms[i] + terms[i + 1] for i in range(0, len(terms), 2)]
    refs[-1][...] = (terms[0] * scale).astype(BF16)


def join_half_kernel(n_gc, *refs):
    out_ref = refs[-1]
    piece = refs[0].shape[0]
    me_gc = lax.axis_index("gc")
    for k in range(n_gc):
        out_ref[pl.ds(pl.multiple_of((me_gc ^ k) * piece, piece), piece)] = refs[k][...]


def join_kernel(mine_ref, other_ref, out_ref):
    half = mine_ref.shape[0]
    core = lax.axis_index("gr") % 2
    out_ref[pl.ds(pl.multiple_of(core * half, half), half)] = mine_ref[...].astype(F32)
    out_ref[pl.ds(pl.multiple_of((1 - core) * half, half), half)] = other_ref[...].astype(F32)


def local(
    out_grad, preactivation_state, features, weight, block_values, block_rows, block_cols, block_counts
):
    n_gr, n_gc = lax.axis_size("gr"), lax.axis_size("gc")
    node_rows, width = out_grad.shape
    block = block_values.shape[-1]
    columns = node_rows * n_gr // block
    per_part = node_rows // block
    (masked,) = mask_rows(out_grad, preactivation_state, block, [width])
    turns = [0, *PART_ORDER] if n_gc == 4 else list(range(n_gc))
    parts = [masked] + [xor_permute(masked, "gc", k) for k in turns[1:]]
    other_features = xor_permute(features, "gr", n_gr // 2)
    lists, values = sort_blocks(
        block_rows[0, 0], block_cols[0, 0], block_counts[0], block_values[0, 0], n_gr, n_gc, per_part
    )
    turned = turn_features(features, other_features)
    early = early_products(lists, values, parts[:-1], turns[:-1], n_gc, columns)
    core_sums, keeps, recvs, products = [], [], [], []
    for j, size in enumerate(WIDTHS):
        after = [turned] if j == TURN_AT else []
        after += products[-1:] + [core_sums[k] for k in CORE_AFTER[j]]
        keep, send = spmm(lists, values, parts[-1], early, sum(WIDTHS[:j]), size, n_gc, columns, after)
        products.append(keep)
        recv = permute_pieces(send, "gr", 1, CORE_PIECES)
        total = (keep.astype(F32) + recv.astype(F32)).astype(BF16)
        core_sums.append(total)
        keeps.append(total[: columns // 4])
        recvs.append(xor_permute(total[columns // 4 :], "gr", 2))
    lows, highs, lasts = [], [], []
    for j in range(len(WIDTHS)):
        low, recv, mask = keeps[j], recvs[j], 2
        while 2 * mask < n_gr:
            if PAIR_AFTER[j]:
                low, high = add_halves(low, recv, [core_sums[k] for k in PAIR_AFTER[j]])
            else:
                total = (low.astype(F32) + recv.astype(F32)).astype(BF16)
                low, high = total[: total.shape[0] // 2], total[total.shape[0] // 2 :]
            mask *= 2
            recv = xor_permute(high, "gr", mask)
        lows.append(low)
        highs.append(high)
        lasts.append(recv)
    others = [lasts[j] if j < W_SPREAD else highs[j] for j in range(len(WIDTHS))]
    kept, sent = weight_terms(lows, others, turned, n_gc)
    half = width // 2
    piece = half // n_gc
    got = xor_permute(sent, "gr", 1)
    own, *sends = small_call(
        functools.partial(split_pieces_kernel, n_gc),
        [((piece, width), F32)] + [((piece, width), BF16)] * (n_gc - 1),
        (kept, got),
        "split_pieces",
        lasts[W_SPREAD:SPLIT_AFTER],
    )
    got = [xor_permute(sends[k - 1], "gc", k) for k in range(1, n_gc)]
    (plane,) = small_call(
        functools.partial(plane_sum_kernel, n_gc),
        [((piece, width), BF16)],
        (own, *got),
        "plane_sum",
        lasts[max(W_SPREAD, SPLIT_AFTER) : PLANE_AFTER],
    )
    terms = [plane] + [xor_permute(plane, "gr", 2 * k) for k in range(1, n_gr // 2)]
    scale = float((node_rows * n_gr * n_gc) ** -0.5)
    (mine,) = small_call(
        functools.partial(column_sum_kernel, len(terms), scale),
        [((piece, width), BF16)],
        terms,
        "column_sum",
    )
    pieces = [mine] + [xor_permute(mine, "gc", k) for k in range(1, n_gc)]
    input_grad = finish(lows, lasts, weight, [mine] if FINISH_LATE else [])
    (joined,) = small_call(
        functools.partial(join_half_kernel, n_gc),
        [((half, width), BF16)],
        pieces,
        "join_half",
        [input_grad] if FINISH_LATE else [],
    )
    other = xor_permute(joined, "gr", 1)
    (weight_grad,) = small_call(join_kernel, [((width, width), F32)], (joined, other), "join")
    return input_grad, weight_grad


def solution(mesh):
    in_specs = (
        P(("gr", "gc"), None),
        P(("gr", "gc"), None),
        P(("gc", "gr"), None),
        P(),
        P("gr", "gc", None, None, None),
        P("gr", "gc", None),
        P("gr", "gc", None),
        P("gr", "gc"),
    )
    out_specs = (P(("gc", "gr"), None), P())
    return jax.shard_map(local, mesh=mesh, in_specs=in_specs, out_specs=out_specs, check_vma=False)
```

```python
import functools

import jax
import jax.numpy as jnp
from jax import lax
from jax.experimental import pallas as pl
from jax.experimental.pallas import tpu as pltpu
from jax.sharding import PartitionSpec as P

QUADS = (4, 2)
UNROLL = 6
WIDTHS = (128, 128, 128, 128)
EARLY_MIB = 24
LATE_MIB = 36
TURN_AT = 1
CORE_PIECES = 1
CORE_AFTER = ((), (), (0,), (1,))
PAIR_AFTER = ((), (2, 3), (), ())
W_SPREAD = 3
PART_ORDER = (1, 2, 3)
SPLIT_AFTER = 0
PLANE_AFTER = 4
FINISH_LATE = False
SORT_MIB = 16
MASK_MIB = 60
VMEM = pl.BlockSpec(memory_space=pltpu.VMEM)
SMEM = pl.BlockSpec(memory_space=pltpu.SMEM)
ANY = pl.BlockSpec(memory_space=pl.ANY)
F32 = jnp.float32
BF16 = jnp.bfloat16


def params(mib=48):
    return pltpu.CompilerParams(vmem_limit_bytes=mib * 2**20)


def xor_permute(array, axis, mask):
    size = lax.axis_size(axis)
    return lax.ppermute(array, axis, [(i, i ^ mask) for i in range(size)])


def permute_pieces(array, axis, mask, pieces):
    step = array.shape[0] // pieces
    parts = [xor_permute(array[i * step : (i + 1) * step], axis, mask) for i in range(pieces)]
    return parts[0] if pieces == 1 else jnp.concatenate(parts, axis=0)


def bit_reversed(index, bits):
    result = 0
    for bit in range(bits):
        result = result + ((index >> bit) & 1) * (1 << (bits - 1 - bit))
    return result


def layout(capacity, columns):
    places, at = [], 0
    for quad in QUADS:
        room = (capacity + columns * (quad - 1)) // quad + UNROLL
        places.append((quad, at, at + room * quad, at + 2 * room * quad, at + (2 * quad + 1) * room))
        at += (2 * quad + 1) * room + 1
    return places, at


def each_block(count, body):
    def step(i, carry):
        for u in range(4):
            body(i * 4 + u, carry)
        return carry

    whole = count >> 2
    lax.fori_loop(0, whole, step, 0)
    lax.fori_loop(whole * 4, count, body, 0)


def sort_kernel(sizes, rows_ref, cols_ref, count_ref, values_hbm, lists_ref, values_ref, place, sem):
    staged = pltpu.make_async_copy(values_hbm, values_ref, sem)
    staged.start()
    n_gr, n_gc, columns, per_part, capacity, bits = sizes
    shift, within = per_part.bit_length() - 1, per_part - 1
    me_gr, me_gc = lax.axis_index("gr"), lax.axis_index("gc")
    count = count_ref[0]
    (early, late), _ = layout(capacity, columns)

    def fill(start, stop, value):
        def put(i, carry):
            lists_ref[i] = value
            return carry

        lax.fori_loop(start, stop, put, 0, unroll=8)

    for _, slots, rows, cols, total in (early, late):
        fill(slots, rows, 0)
        fill(rows, cols, n_gc * per_part)
        fill(cols, total, columns)

    def clear(c, carry):
        place[c] = 0
        return carry

    lax.fori_loop(0, 2 * columns, clear, 0, unroll=8)

    def cell(s):
        part = (rows_ref[s] >> shift) ^ me_gc
        is_late = part == n_gc - 1
        return part, is_late, jnp.where(is_late, columns, 0) + cols_ref[s]

    def tally(s, carry):
        _, _, c = cell(s)
        place[c] = place[c] + 1
        return carry

    each_block(count, tally)

    for which, (quad, _, _, _, total) in enumerate((early, late)):
        first = which * columns

        def open_column(c, group, first=first, quad=quad):
            held = place[first + c]
            place[first + c] = group * quad
            return group + ((held + quad - 1) >> (quad.bit_length() - 1))

        lists_ref[total] = lax.fori_loop(0, columns, open_column, 0, unroll=4)

    def insert(s, carry):
        part, is_late, c = cell(s)
        at = place[c]
        place[c] = at + 1
        col = cols_ref[s]
        quad, slots, rows, cols = [jnp.where(is_late, late[i], early[i]) for i in range(4)]
        lists_ref[slots + at] = s
        lists_ref[rows + at] = (part << shift) | (rows_ref[s] & within)
        down = jnp.where(is_late, QUADS[1].bit_length() - 1, QUADS[0].bit_length() - 1)
        home = bit_reversed((col >> shift) ^ me_gr, bits)
        lists_ref[cols + (at >> down)] = (home << shift) | (col & within)
        return carry

    each_block(count, insert)
    staged.wait()


def sort_blocks(rows, cols, count, values, n_gr, n_gc, per_part):
    capacity = rows.shape[0]
    columns = n_gr * per_part
    bits = n_gr.bit_length() - 1
    sizes = (n_gr, n_gc, columns, per_part, capacity, bits)
    return pl.pallas_call(
        functools.partial(sort_kernel, sizes),
        out_shape=(
            jax.ShapeDtypeStruct((layout(capacity, columns)[1],), jnp.int32),
            jax.ShapeDtypeStruct(values.shape, BF16),
        ),
        in_specs=[SMEM, SMEM, SMEM, ANY],
        out_specs=(SMEM, VMEM),
        scratch_shapes=[pltpu.SMEM((2 * columns,), jnp.int32), pltpu.SemaphoreType.DMA],
        compiler_params=params(SORT_MIB),
        name="sort_blocks",
    )(rows, cols, count, values)


def mask_kernel(grad_hbm, state_hbm, *refs):
    out_refs, (grad, state, sems) = refs[:-3], refs[-3:]
    blocks, _, block = out_refs[0].shape
    copies = []
    for b in range(blocks):
        rows = pl.ds(b * block, block)
        copies.append(
            [
                pltpu.make_async_copy(grad_hbm.at[rows], grad.at[rows], sems.at[0, b]),
                pltpu.make_async_copy(state_hbm.at[rows], state.at[rows], sems.at[1, b]),
            ]
        )
    for pair in copies:
        for copy in pair:
            copy.start()
    for b in range(blocks):
        for copy in copies[b]:
            copy.wait()
        held = grad[b * block : (b + 1) * block]
        masked = jnp.where(state[b * block : (b + 1) * block] > 0, held, jnp.zeros_like(held))
        at = 0
        for out_ref in out_refs:
            width = out_ref.shape[1]
            out_ref[b] = masked[:, at : at + width].T
            at += width


def mask_rows(out_grad, state, block, widths):
    blocks = out_grad.shape[0] // block
    return pl.pallas_call(
        mask_kernel,
        out_shape=tuple(jax.ShapeDtypeStruct((blocks, width, block), BF16) for width in widths),
        in_specs=[ANY, ANY],
        out_specs=(VMEM,) * len(widths),
        scratch_shapes=[
            pltpu.VMEM(out_grad.shape, BF16),
            pltpu.VMEM(out_grad.shape, BF16),
            pltpu.SemaphoreType.DMA((2, blocks)),
        ],
        compiler_params=params(MASK_MIB),
        name="mask_rows",
    )(out_grad, state)


def turn_kernel(own_ref, other_ref, out_ref):
    rows = own_ref.shape[0]
    out_ref[:, :rows] = own_ref[...].T
    out_ref[:, rows:] = other_ref[...].T


def turn_features(own, other):
    rows, width = own.shape
    (result,) = small_call(turn_kernel, [((width, 2 * rows), BF16)], (own, other), "turn_features")
    return result


def weight_kernel(n_gc, n_chunks, *refs):
    lows, others, (turned_ref, kept_ref, sent_ref, term) = (
        refs[:n_chunks], refs[n_chunks : 2 * n_chunks], refs[2 * n_chunks :]
    )
    at = 0
    for j, (low, other) in enumerate(zip(lows, others)):
        blocks = range(low.shape[0])
        if j < W_SPREAD:
            tiles = [(low[b].astype(F32) + other[b].astype(F32)).astype(BF16) for b in blocks]
        else:
            tiles = [ref[b] for ref in (low, other) for b in blocks]
        right = jnp.concatenate(tiles, axis=1)
        width, nodes = right.shape
        term[:, at : at + width] = lax.dot_general(
            turned_ref[:, :nodes], right, (((1,), (1,)), ((), ())), preferred_element_type=F32
        )
        at += width
    core, me_gc = lax.axis_index("gr") % 2, lax.axis_index("gc")
    piece = kept_ref.shape[0] // n_gc
    for k in range(n_gc):
        here = pl.multiple_of((core * n_gc + (me_gc ^ k)) * piece, piece)
        there = pl.multiple_of(((1 - core) * n_gc + (me_gc ^ k)) * piece, piece)
        kept_ref[k * piece : (k + 1) * piece] = term[pl.ds(here, piece)]
        sent_ref[k * piece : (k + 1) * piece] = term[pl.ds(there, piece)].astype(BF16)


def weight_terms(lows, others, turned, n_gc):
    width = turned.shape[0]
    out_width = sum(low.shape[1] for low in lows)
    return pl.pallas_call(
        functools.partial(weight_kernel, n_gc, len(lows)),
        out_shape=(
            jax.ShapeDtypeStruct((width // 2, out_width), F32),
            jax.ShapeDtypeStruct((width // 2, out_width), BF16),
        ),
        in_specs=[VMEM] * (2 * len(lows) + 1),
        out_specs=(VMEM,) * 2,
        scratch_shapes=[pltpu.VMEM((width, out_width), F32)],
        compiler_params=params(16),
        name="weight_terms",
    )(*lows, *others, turned)


def add_products(which, list_ref, values_ref, stacked, total):
    quad, slots_at, rows_at, cols_at, count_at = layout(values_ref.shape[0], total.shape[0] - 1)[0][which]

    def step(i, carry):
        products = []
        for u in range(UNROLL):
            at = (i * UNROLL + u) * quad
            left = jnp.concatenate([stacked[list_ref[rows_at + at + j]] for j in range(quad)], axis=1)
            right = jnp.concatenate([values_ref[list_ref[slots_at + at + j]] for j in range(quad)], axis=0)
            products.append(jnp.dot(left, right, preferred_element_type=F32))
        for u in range(UNROLL):
            place = list_ref[cols_at + i * UNROLL + u]
            total[place] = total[place] + products[u]
        return carry

    lax.fori_loop(0, (list_ref[count_at] + UNROLL - 1) // UNROLL, step, 0)


def early_kernel(turns, list_ref, values_ref, *refs):
    parts, (total, stacked) = refs[: len(turns)], refs[-2:]
    part_blocks = parts[0].shape[0]
    for k, part in zip(turns, parts):
        stacked[k * part_blocks : (k + 1) * part_blocks] = part[...]
    stacked[stacked.shape[0] - 1] = jnp.zeros(stacked.shape[1:], BF16)
    total[...] = jnp.zeros_like(total)
    add_products(0, list_ref, values_ref, stacked, total)


def early_products(blocks, values, parts, turns, n_gc, columns):
    part_blocks, width, block = parts[0].shape
    return pl.pallas_call(
        functools.partial(early_kernel, turns),
        out_shape=jax.ShapeDtypeStruct((columns + 1, width, block), F32),
        in_specs=[SMEM] + [VMEM] * (len(parts) + 1),
        out_specs=VMEM,
        scratch_shapes=[pltpu.VMEM((n_gc * part_blocks + 1, width, block), BF16)],
        compiler_params=params(EARLY_MIB),
        name="early_products",
    )(blocks, values, *parts)


def spmm_kernel(start, list_ref, values_ref, part_ref, early_ref, *refs):
    keep_ref, send_ref, stacked, total = refs[-4:]
    width = total.shape[1]
    part_blocks = part_ref.shape[0]
    half = keep_ref.shape[0]
    total[...] = early_ref[:, start : start + width]
    last = stacked.shape[0] - 1
    stacked[last - part_blocks : last] = part_ref[:, start : start + width]
    stacked[last] = jnp.zeros(stacked.shape[1:], BF16)
    add_products(1, list_ref, values_ref, stacked, total)
    keep_ref[...] = total[:half].astype(BF16)
    send_ref[...] = total[half : 2 * half].astype(BF16)


def spmm(blocks, values, part, early, start, width, n_gc, columns, after=()):
    part_blocks, _, block = part.shape
    half = jax.ShapeDtypeStruct((columns // 2, width, block), BF16)
    return pl.pallas_call(
        functools.partial(spmm_kernel, start),
        out_shape=(half, half),
        in_specs=[SMEM, VMEM, VMEM, VMEM] + [ANY] * len(after),
        out_specs=(VMEM, VMEM),
        scratch_shapes=[
            pltpu.VMEM((n_gc * part_blocks + 1, width, block), BF16),
            pltpu.VMEM((columns + 1, width, block), F32),
        ],
        compiler_params=params(LATE_MIB),
        name="tile_partial",
    )(blocks, values, part, early, *after)


def add_kernel(keep_ref, recv_ref, *refs):
    low_ref, high_ref = refs[-2:]
    half = low_ref.shape[0]
    low_ref[...] = (keep_ref[:half].astype(F32) + recv_ref[:half].astype(F32)).astype(BF16)
    high_ref[...] = (keep_ref[half:].astype(F32) + recv_ref[half:].astype(F32)).astype(BF16)


def add_halves(keep, recv, after):
    half = (keep.shape[0] // 2, *keep.shape[1:])
    return small_call(add_kernel, [(half, BF16)] * 2, (keep, recv), "add_halves", after)


def finish_kernel(n_chunks, *refs):
    keeps, recvs = refs[:n_chunks], refs[n_chunks : 2 * n_chunks]
    weight_ref, input_grad_ref, spread = refs[2 * n_chunks], *refs[-2:]
    at = 0
    for keep, recv in zip(keeps, recvs):
        blocks, width, block = keep.shape
        for b in range(blocks):
            tile = (keep[b].astype(F32) + recv[b].astype(F32)).astype(BF16)
            spread[b * block : (b + 1) * block, at : at + width] = tile.T
        at += width
    input_grad_ref[...] = lax.dot_general(
        spread[...], weight_ref[...], (((1,), (1,)), ((), ())), preferred_element_type=F32
    ).astype(BF16)


def finish(keeps, recvs, weight, after):
    blocks, _, block = keeps[0].shape
    rows = blocks * block
    return pl.pallas_call(
        functools.partial(finish_kernel, len(keeps)),
        out_shape=jax.ShapeDtypeStruct((rows, weight.shape[0]), BF16),
        in_specs=[VMEM] * (2 * len(keeps) + 1) + [ANY] * len(after),
        out_specs=VMEM,
        scratch_shapes=[pltpu.VMEM((rows, weight.shape[1]), BF16)],
        compiler_params=params(16),
        name="finish",
    )(*keeps, *recvs, weight, *after)


def small_call(kernel, outs, args, name, after=()):
    return pl.pallas_call(
        kernel,
        out_shape=tuple(jax.ShapeDtypeStruct(s, d) for s, d in outs),
        in_specs=[VMEM] * len(args) + [ANY] * len(after),
        out_specs=(VMEM,) * len(outs),
        compiler_params=params(16),
        name=name,
    )(*args, *after)


def split_pieces_kernel(n_gc, kept_ref, got_ref, *refs):
    own_ref, *send_refs = refs[-n_gc:]
    piece = own_ref.shape[0]
    own_ref[...] = kept_ref[:piece] + got_ref[:piece].astype(F32)
    for k in range(1, n_gc):
        here = slice(k * piece, (k + 1) * piece)
        send_refs[k - 1][...] = (kept_ref[here] + got_ref[here].astype(F32)).astype(BF16)


def plane_sum_kernel(terms, own_ref, *refs):
    total = own_ref[...]
    for ref in refs[: terms - 1]:
        total = total + ref[...].astype(F32)
    refs[-1][...] = total.astype(BF16)


def column_sum_kernel(count, scale, *refs):
    terms = [ref[...].astype(F32) for ref in refs[:count]]
    while len(terms) > 1:
        terms = [terms[i] + terms[i + 1] for i in range(0, len(terms), 2)]
    refs[-1][...] = (terms[0] * scale).astype(BF16)


def join_half_kernel(n_gc, *refs):
    out_ref = refs[-1]
    piece = refs[0].shape[0]
    me_gc = lax.axis_index("gc")
    for k in range(n_gc):
        out_ref[pl.ds(pl.multiple_of((me_gc ^ k) * piece, piece), piece)] = refs[k][...]


def join_kernel(mine_ref, other_ref, out_ref):
    half = mine_ref.shape[0]
    core = lax.axis_index("gr") % 2
    out_ref[pl.ds(pl.multiple_of(core * half, half), half)] = mine_ref[...].astype(F32)
    out_ref[pl.ds(pl.multiple_of((1 - core) * half, half), half)] = other_ref[...].astype(F32)


def local(
    out_grad, preactivation_state, features, weight, block_values, block_rows, block_cols, block_counts
):
    n_gr, n_gc = lax.axis_size("gr"), lax.axis_size("gc")
    node_rows, width = out_grad.shape
    block = block_values.shape[-1]
    columns = node_rows * n_gr // block
    per_part = node_rows // block
    (masked,) = mask_rows(out_grad, preactivation_state, block, [width])
    turns = [0, *PART_ORDER] if n_gc == 4 else list(range(n_gc))
    parts = [masked] + [xor_permute(masked, "gc", k) for k in turns[1:]]
    other_features = xor_permute(features, "gr", n_gr // 2)
    lists, values = sort_blocks(
        block_rows[0, 0], block_cols[0, 0], block_counts[0], block_values[0, 0], n_gr, n_gc, per_part
    )
    turned = turn_features(features, other_features)
    early = early_products(lists, values, parts[:-1], turns[:-1], n_gc, columns)
    core_sums, keeps, recvs, products = [], [], [], []
    for j, size in enumerate(WIDTHS):
        after = [turned] if j == TURN_AT else []
        after += products[-1:] + [core_sums[k] for k in CORE_AFTER[j]]
        keep, send = spmm(lists, values, parts[-1], early, sum(WIDTHS[:j]), size, n_gc, columns, after)
        products.append(keep)
        recv = permute_pieces(send, "gr", 1, CORE_PIECES)
        total = (keep.astype(F32) + recv.astype(F32)).astype(BF16)
        core_sums.append(total)
        keeps.append(total[: columns // 4])
        recvs.append(xor_permute(total[columns // 4 :], "gr", 2))
    lows, highs, lasts = [], [], []
    for j in range(len(WIDTHS)):
        low, recv, mask = keeps[j], recvs[j], 2
        while 2 * mask < n_gr:
            if PAIR_AFTER[j]:
                low, high = add_halves(low, recv, [core_sums[k] for k in PAIR_AFTER[j]])
            else:
                total = (low.astype(F32) + recv.astype(F32)).astype(BF16)
                low, high = total[: total.shape[0] // 2], total[total.shape[0] // 2 :]
            mask *= 2
            recv = xor_permute(high, "gr", mask)
        lows.append(low)
        highs.append(high)
        lasts.append(recv)
    others = [lasts[j] if j < W_SPREAD else highs[j] for j in range(len(WIDTHS))]
    kept, sent = weight_terms(lows, others, turned, n_gc)
    half = width // 2
    piece = half // n_gc
    got = xor_permute(sent, "gr", 1)
    own, *sends = small_call(
        functools.partial(split_pieces_kernel, n_gc),
        [((piece, width), F32)] + [((piece, width), BF16)] * (n_gc - 1),
        (kept, got),
        "split_pieces",
        lasts[W_SPREAD:SPLIT_AFTER],
    )
    got = [xor_permute(sends[k - 1], "gc", k) for k in range(1, n_gc)]
    (plane,) = small_call(
        functools.partial(plane_sum_kernel, n_gc),
        [((piece, width), BF16)],
        (own, *got),
        "plane_sum",
        lasts[max(W_SPREAD, SPLIT_AFTER) : PLANE_AFTER],
    )
    terms = [plane] + [xor_permute(plane, "gr", 2 * k) for k in range(1, n_gr // 2)]
    scale = float((node_rows * n_gr * n_gc) ** -0.5)
    (mine,) = small_call(
        functools.partial(column_sum_kernel, len(terms), scale),
        [((piece, width), BF16)],
        terms,
        "column_sum",
    )
    pieces = [mine] + [xor_permute(mine, "gc", k) for k in range(1, n_gc)]
    input_grad = finish(lows, lasts, weight, [mine] if FINISH_LATE else [])
    (joined,) = small_call(
        functools.partial(join_half_kernel, n_gc),
        [((half, width), BF16)],
        pieces,
        "join_half",
        [input_grad] if FINISH_LATE else [],
    )
    other = xor_permute(joined, "gr", 1)
    (weight_grad,) = small_call(join_kernel, [((width, width), F32)], (joined, other), "join")
    return input_grad, weight_grad


def solution(mesh):
    in_specs = (
        P(("gr", "gc"), None),
        P(("gr", "gc"), None),
        P(("gc", "gr"), None),
        P(),
        P("gr", "gc", None, None, None),
        P("gr", "gc", None),
        P("gr", "gc", None),
        P("gr", "gc"),
    )
    out_specs = (P(("gc", "gr"), None), P())
    return jax.shard_map(local, mesh=mesh, in_specs=in_specs, out_specs=out_specs, check_vma=False)
```
